128 devices in a mesh: curve: 128 (over x, y, z, core).
Axes of the slice: x: 4, y: 4, z: 4, core: 2. Of those that a mesh axis runs over, the one named last changes fastest.
Arguments:
- sea_state: float32 [3, 25, 131072], P(None, None, 'curve'), may hold values from -6 to 6
- water_depth: float32 [25, 131072], P(None, 'curve'), may hold values from 0.25 to 4
- neighbours: int32 [4, 131072], P(None, 'curve'), may hold values from -1 to 1023, as said below
- neighbour_owner: int32 [4, 131072], P(None, 'curve'), may hold values from -1 to 127, as said below
- clusters: int32 [131072], P('curve'), may hold values from 0 to 1, as said below
- block_swap: int32 [4096], P('curve'), may hold values from 0 to 1, as said below
Outputs:
- moved_state: float32 [3, 25, 131072], P(None, None, 'curve')
The draws below stay inside these ranges and needn't reach their ends.
Inputs may be any that keep to these rules, and one draw needn't show every extreme that they name: Entry f of a cell is the position, within its owner's block, of its neighbour across face f (0 west, 1 east, 2 south, 3 north), -1 at a wall or the domain's edge; if a names b across face f, b names a across face f xor 1. Cell l of a device lies at row l // 32 and column l % 32 of the device's square block; faces between blocks of two devices are never walls; the cells along one edge of a block have their neighbours beyond it on one device, another one for each edge. `neighbour_owner`: entry f is the device that holds the neighbour across face f, -1 exactly where neighbours is -1. A neighbour on another device lies 1 or 64 devices away along the curve, and both distances occur. `clusters`: 0: the cell takes two half steps; 1: one whole step. `block_swap`: A block and its partner carry the same value; it is 0 where the partner would lie outside the curve.
All inputs are finite; a program needn't handle non-finite values.
Results may differ from the reference program's by a relative error of at most 0.0001.
Values sent between devices are 32-bit elements; how exact they have to be, the bound alone decides.
No kernel may reach another device: no remote copies, remote signals or barrier semaphores. Data moves between devices by JAX's collectives and lax.ppermute only.
A program may use at most 64 MiB of HBM per device.

```python
import math
import jax
import jax.numpy as jnp
import numpy as np
from jax import lax

VARS = 3
NODES = 25
BS = 32
PX = 64
SLOTS = 1024
TOTAL = 131072
BLOCKS = 4096


def neighbour_grid(key):
    devices = TOTAL // SLOTS
    grid_width = PX * BS
    grid_height = devices // PX * BS
    cell_index = jnp.arange(TOTAL, dtype=jnp.int32)
    device = cell_index // SLOTS
    local_index = cell_index % SLOTS
    block_row = device // PX
    block_column = device % PX
    cell_column = block_column * BS + local_index % BS
    cell_row = block_row * BS + local_index // BS
    east_walls = (jax.random.randint(jax.random.fold_in(key, 21), (grid_height, grid_width), 0, 8) == 0) & (jnp.arange(grid_width)[None, :] % BS != BS - 1)
    north_walls = (jax.random.randint(jax.random.fold_in(key, 22), (grid_height, grid_width), 0, 8) == 0) & (jnp.arange(grid_height)[:, None] % BS != BS - 1)

    def locate(column_at, row_at):
        row_block = row_at // BS
        column_block = column_at // BS
        return (row_block * PX + column_block) * SLOTS + row_at % BS * BS + column_at % BS
    left_column = jnp.maximum(cell_column - 1, 0)
    right_column = jnp.minimum(cell_column + 1, grid_width - 1)
    lower_row = jnp.maximum(cell_row - 1, 0)
    upper_row = jnp.minimum(cell_row + 1, grid_height - 1)
    west_face = jnp.where((cell_column > 0) & ~east_walls[cell_row, left_column], locate(left_column, cell_row), -1)
    east_face = jnp.where((cell_column < grid_width - 1) & ~east_walls[cell_row, cell_column], locate(right_column, cell_row), -1)
    south_face = jnp.where((cell_row > 0) & ~north_walls[lower_row, cell_column], locate(cell_column, lower_row), -1)
    north_face = jnp.where((cell_row < grid_height - 1) & ~north_walls[cell_row, cell_column], locate(cell_column, upper_row), -1)
    return jnp.stack([west_face, east_face, south_face, north_face]).astype(jnp.int32)


def draw_neighbours(key, part):
    whole = neighbour_grid(key)
    return jnp.where(whole < 0, -1, whole % SLOTS).astype(jnp.int32)


def draw_neighbour_owner(key, part):
    whole = neighbour_grid(key)
    return jnp.where(whole < 0, -1, whole // SLOTS).astype(jnp.int32)


def draw_clusters(key, part):
    key = jax.random.fold_in(key, 12)
    devices = TOTAL // SLOTS
    fine_share = jax.random.randint(jax.random.fold_in(key, 1), (devices,), 1, 8)
    coin_draw = jax.random.randint(jax.random.fold_in(key, 2), (TOTAL,), 0, 8)
    cell_device = jnp.arange(TOTAL, dtype=jnp.int32) // SLOTS
    return jnp.where(coin_draw < fine_share[cell_device], 0, 1).astype(jnp.int32)


def draw_block_swap(key, part):
    key = jax.random.fold_in(key, 13)
    devices = TOTAL // SLOTS
    block_index = jnp.arange(BLOCKS, dtype=jnp.int32)
    block_owner = block_index // BS
    position = block_index % BS
    lower_device = jnp.where((block_owner + position) % 2 == 0, block_owner, block_owner - 1)
    coin_flips = jax.random.randint(key, (BLOCKS,), 0, 2)
    picked = coin_flips[jnp.clip(lower_device, 0, devices - 1) * BS + position]
    inside_curve = (lower_device >= 0) & (lower_device + 1 < devices)
    return jnp.where(inside_curve, picked, 0).astype(jnp.int32)


def level_of(stream_key, extent, pieces, smallest, high):
    def one(dim, blocks):
        steps = jax.random.uniform(jax.random.fold_in(jax.random.fold_in(stream_key, 6), dim), (blocks,), jnp.float32, smallest / len(pieces), high / len(pieces))
        return jnp.repeat(jnp.exp(steps), extent[dim] // blocks).reshape((-1,) + (1,) * (len(extent) - dim - 1))

    level = one(*pieces[0])
    for cut in pieces[1:]:
        level = level * one(*cut)
    return level


def centred(key, shape, deviation, bound, shards=(), kind=jnp.bfloat16):
    values = deviation * jax.random.normal(key, shape, jnp.float32)
    if shards:
        values = values * level_of(key, shape, shards, -0.22, 0.18)
    return jnp.clip(values, -bound, bound).astype(kind)


def setup_inputs(seed: int = 0) -> dict:
    keys = jax.random.split(jax.random.key(seed), 7)
    sea_state = centred(keys[0], (VARS, NODES, TOTAL), 1.0, 6.0, ((2, 128),), jnp.float32)
    water_depth = jnp.clip(jnp.exp(math.log(4.0) - 2.7725887 * jax.random.uniform(keys[1], (NODES, TOTAL), jnp.float32) ** level_of(keys[1], (NODES, TOTAL), ((1, 128),), -0.2, 0.2)), 0.25, 4.0)
    neighbours = draw_neighbours(jax.random.fold_in(keys[6], 71), 0)
    neighbour_owner = draw_neighbour_owner(jax.random.fold_in(keys[6], 71), 0)
    clusters = draw_clusters(jax.random.fold_in(keys[6], 71), 0)
    block_swap = draw_block_swap(jax.random.fold_in(keys[6], 71), 0)
    return {"sea_state": sea_state, "water_depth": water_depth, "neighbours": neighbours, "neighbour_owner": neighbour_owner, "clusters": clusters, "block_swap": block_swap}


LAMBDA_STEP = 0.06
LIFT_SCALE = 10.0
HIGHEST = lax.Precision.HIGHEST
FACE_NODES = ((0, 5, 10, 15, 20), (4, 9, 14, 19, 24), (0, 1, 2, 3, 4), (20, 21, 22, 23, 24))
NORMALS = ((-1.0, 0.0), (1.0, 0.0), (0.0, -1.0), (0.0, 1.0))

def derivative_matrix():
    points = np.array([-1.0, -np.sqrt(3.0 / 7.0), 0.0, np.sqrt(3.0 / 7.0), 1.0])
    weights = []
    for column in range(5):
        product = 1.0
        for other_point in range(5):
            if other_point != column:
                product = product * (points[column] - points[other_point])
        weights.append(1.0 / product)
    matrix = np.zeros((5, 5))
    for row_index in range(5):
        for column in range(5):
            if row_index != column:
                matrix[row_index, column] = weights[column] / weights[row_index] / (points[row_index] - points[column])
        matrix[row_index, row_index] = -np.sum(matrix[row_index])
    return matrix

def operator_tables():
    deriv_small = derivative_matrix()
    identity = np.eye(5)
    lift_table = np.zeros((4, 25, 5))
    for face_index in range(4):
        for node_index in range(5):
            lift_table[face_index, FACE_NODES[face_index][node_index], node_index] = 1.0
    deriv_x = jnp.asarray(np.kron(identity, deriv_small), dtype=jnp.float32)
    deriv_y = jnp.asarray(np.kron(deriv_small, identity), dtype=jnp.float32)
    return (deriv_x, deriv_y, jnp.asarray(lift_table, dtype=jnp.float32))

def face_trace(values_in, face_index):
    if face_index == 0:
        return values_in[..., 0::5, :]
    if face_index == 1:
        return values_in[..., 4::5, :]
    if face_index == 2:
        return values_in[..., 0:5, :]
    return values_in[..., 20:25, :]

def product_of(matrix, field):
    return jnp.dot(matrix, field, preferred_element_type=jnp.float32, precision=HIGHEST)

def operate(fields, water_depth, deriv_x, deriv_y):
    grad_x = product_of(deriv_x, fields[0])
    grad_y = product_of(deriv_y, fields[0])
    spread = product_of(deriv_x, fields[1]) + product_of(deriv_y, fields[2])
    return -LAMBDA_STEP * jnp.stack([spread, water_depth * grad_x, water_depth * grad_y])

def taylor_list(fields, water_depth, deriv_x, deriv_y):
    result = [fields]
    for term_order in range(3):
        result.append(operate(result[-1], water_depth, deriv_x, deriv_y))
    return result

def integrate(taylor_terms, time_start, time_end):
    accumulated = jnp.zeros_like(taylor_terms[0])
    for term_order in range(4):
        factor = (time_end ** (term_order + 1) - time_start ** (term_order + 1)) / math.factorial(term_order + 1)
        accumulated = accumulated + factor * taylor_terms[term_order]
    return accumulated

def surface_term(fields, outer_list, water_depth, depth_list, wall_mask, lift_table):
    accumulated = jnp.zeros_like(fields)
    for face_index in range(4):
        normal_x, normal_y = NORMALS[face_index]
        inner_trace = face_trace(fields, face_index)
        depth_inner = face_trace(water_depth, face_index)
        mirror = jnp.stack([inner_trace[0], inner_trace[1] * (1.0 - 2.0 * abs(normal_x)), inner_trace[2] * (1.0 - 2.0 * abs(normal_y))])
        outer_trace = jnp.where(wall_mask[face_index][None, None, :], mirror, outer_list[face_index])
        depth_outer = jnp.where(wall_mask[face_index][None, :], depth_inner, depth_list[face_index])
        wave_speed = jnp.sqrt(jnp.maximum(depth_inner, depth_outer))
        trace_jump = outer_trace - inner_trace
        jump_normal = trace_jump[1] * normal_x + trace_jump[2] * normal_y
        correction = LAMBDA_STEP * LIFT_SCALE * 0.5 * jnp.stack([wave_speed * trace_jump[0] - jump_normal, wave_speed * trace_jump[1] - depth_inner * trace_jump[0] * normal_x, wave_speed * trace_jump[2] - depth_inner * trace_jump[0] * normal_y])
        accumulated = accumulated + jnp.einsum('nk,vkc->vnc', lift_table[face_index], correction, precision=HIGHEST)
    return accumulated

def neighbour_values(values_in, neighbours):
    result = []
    for face_index in range(4):
        safe_index = jnp.maximum(neighbours[face_index], 0)
        result.append(jnp.take(face_trace(values_in, face_index ^ 1), safe_index, axis=-1))
    return result

def migrate(updated, block_swap):
    blocks = block_swap.shape[0]
    block_index = jnp.arange(blocks, dtype=jnp.int32)
    block_owner = block_index // BS
    position = block_index % BS
    partner = jnp.where((block_owner + position) % 2 == 0, block_index + BS, block_index - BS)
    source = jnp.where(block_swap > 0, partner, block_index).astype(jnp.int32)
    grouped = updated.reshape(3, 25, blocks, BS)
    return jnp.take(grouped, source, axis=2).reshape(updated.shape)

def reference(sea_state, water_depth, neighbours, neighbour_owner, clusters, block_swap):
    deriv_x, deriv_y, lift_table = operator_tables()
    global_index = jnp.where(neighbours < 0, -1, jnp.maximum(neighbour_owner, 0) * SLOTS + jnp.maximum(neighbours, 0)).astype(jnp.int32)
    wall_mask = [neighbours[face_index] < 0 for face_index in range(4)]
    fine_mask = (clusters == 0)[None, None, :]
    taylor_terms = taylor_list(sea_state, water_depth, deriv_x, deriv_y)
    first_half = integrate(taylor_terms, 0.0, 0.5)
    second_half = integrate(taylor_terms, 0.5, 1.0)
    near_depth = neighbour_values(water_depth, global_index)
    near_first = neighbour_values(first_half, global_index)
    middle = sea_state + operate(first_half, water_depth, deriv_x, deriv_y) + surface_term(first_half, near_first, water_depth, near_depth, wall_mask, lift_table)
    late_half = integrate(taylor_list(middle, water_depth, deriv_x, deriv_y), 0.0, 0.5)
    sent_late = jnp.where(fine_mask, late_half, second_half)
    near_late = neighbour_values(sent_late, global_index)
    fine_state = middle + operate(late_half, water_depth, deriv_x, deriv_y) + surface_term(late_half, near_late, water_depth, near_depth, wall_mask, lift_table)
    whole_step = first_half + second_half
    near_whole = [near_first[face_index] + near_late[face_index] for face_index in range(4)]
    coarse_state = sea_state + operate(whole_step, water_depth, deriv_x, deriv_y) + surface_term(whole_step, near_whole, water_depth, near_depth, wall_mask, lift_table)
    updated = jnp.where(fine_mask, fine_state, coarse_state)
    return migrate(updated, block_swap)
```

```python
import math

import jax
import jax.numpy as jnp
import numpy as np
from jax import lax
from jax.experimental import pallas as pl
from jax.experimental.pallas import tpu as pltpu
from jax.sharding import PartitionSpec as P

F32 = jnp.float32
FACES = ((0, 5, 10, 15, 20), (4, 9, 14, 19, 24), (0, 1, 2, 3, 4), (20, 21, 22, 23, 24))
EDGE = tuple(sorted({n for face in FACES for n in face}))
PLACE = {n: i for i, n in enumerate(EDGE)}
LIFT = 0.06 * 10.0 * 0.5
HALF = [0.5 ** (k + 1) / math.factorial(k + 1) for k in range(4)]
WHOLE = [1.0 / math.factorial(k + 1) for k in range(4)]
AT_DEPTH, AT_FLAG, AT_X, AT_X2, AT_Y, AT_Y2, PLANES = 75, 100, 104, 120, 136, 152, 168
IN_FACE, IN_SECOND, IN_SIDE, IN_ALL = 104, 120, 136, 152
VALUES = [i for i in range(IN_ALL) if i < 101 or (i >= 104 and (i - 104) % 16 < 15)]


def derivative_matrix():
    points = np.array([-1.0, -np.sqrt(3.0 / 7.0), 0.0, np.sqrt(3.0 / 7.0), 1.0])
    gaps = points[:, None] - points[None, :] + np.eye(5)
    weights = 1.0 / gaps.prod(axis=1)
    matrix = weights[None, :] / weights[:, None] / gaps
    matrix -= np.diag(np.diag(matrix))
    return matrix - np.diag(matrix.sum(axis=1))


STEP = -0.06 * derivative_matrix()


def slope(f):
    even_a, even_b, odd_a, odd_b = f[0] + f[4], f[1] + f[3], f[0] - f[4], f[1] - f[3]
    twice = f[2] + f[2]
    even_a, even_b = even_a - twice, even_b - twice
    out = [None] * 5
    for i in (0, 1):
        minus = float(STEP[i, 0] + STEP[i, 4]) * 0.5 * even_a + float(STEP[i, 1] + STEP[i, 3]) * 0.5 * even_b
        plus = float(STEP[i, 0] - STEP[i, 4]) * 0.5 * odd_a + float(STEP[i, 1] - STEP[i, 3]) * 0.5 * odd_b
        out[i], out[4 - i] = plus + minus, plus - minus
    out[2] = float(STEP[2, 0]) * odd_a + float(STEP[2, 1]) * odd_b
    return out


def operate(src, dst, depth):
    spread = [None] * 25
    for j in range(5):
        line = [5 * j + i for i in range(5)]
        grad = slope([src[n] for n in line])
        part = slope([src[25 + n] for n in line])
        for i, n in enumerate(line):
            dst[25 + n] = depth(n) * grad[i]
            dst[n] = part[i]
    for i in range(5):
        line = [5 * j + i for j in range(5)]
        grad = slope([src[n] for n in line])
        part = slope([src[50 + n] for n in line])
        for j, n in enumerate(line):
            dst[50 + n] = depth(n) * grad[j]
            dst[n] = dst[n] + part[j]


def weighted(values, weights):
    total = weights[0] * values[0]
    for value, weight in zip(values[1:], weights[1:]):
        total = total + weight * value
    return total


def lanes(x, by):
    return x if by % 128 == 0 else pltpu.roll(x, by % 128, 1)


def subs(x, by):
    return pltpu.roll(x, by % 8, 0)


class Grid:
    def __init__(self):
        self.lane = lax.broadcasted_iota(jnp.int32, (8, 128), 1)
        self.sub = lax.broadcasted_iota(jnp.int32, (8, 128), 0)
        self.col = self.lane % 32
        self.west = self.col < 16
        self.south = self.sub < 4

    def across(self, x, face):
        if face == 0:
            return lanes(x, 1)
        if face == 1:
            return lanes(x, -1)
        if face == 2:
            y = lanes(x, 32)
            return jnp.where(self.lane < 32, subs(y, 1), y)
        y = lanes(x, -32)
        return jnp.where(self.lane >= 96, subs(y, -1), y)


def spread_ints(ref, out):
    for j in range(8):
        out[:, j, :] = ref[:, 128 * j : 128 * j + 128]


def face_facts(near, owner):
    me = lax.axis_index("curve")
    odd = me % 2
    chip = me + 1 - 2 * odd
    swap = me - 1 + 2 * odd
    walls, remotes, slots = [], [], []
    for f in range(4):
        wall = near[f] < 0
        remote = (near[f] >= 0) & (owner[f] != me)
        peer = jnp.max(jnp.where(remote, owner[f], -1).astype(F32)).astype(jnp.int32)
        walls.append(wall)
        remotes.append(remote)
        slot = jnp.where(peer == chip, 0, jnp.where(peer == swap, 1, 2))
        slots.append(jnp.where(peer < 0, 3, slot))
    return walls, remotes, slots


def flux(js, jn, jt, speed, depth, sign):
    lifted = LIFT * speed
    turn = LIFT * sign
    return lifted * js - turn * jn, lifted * jn - depth * (turn * js), lifted * jt


def first_kernel(sea, dep, near_in, owner_in, cl, ex, eo, es, dg, ps, cb, tr1, tr2, nf, cc, u, near, owner):
    grid = Grid()
    lane, sub, col = grid.lane, grid.sub, grid.col
    spread_ints(near_in, near)
    spread_ints(owner_in, owner)
    walls, remotes, slots = face_facts(near, owner)
    inner = [~(walls[f] | remotes[f]) for f in range(4)]
    u[0] = sea[...].reshape(75, 8, 128)
    ps[8 * AT_DEPTH : 8 * AT_FLAG, :] = dep[...].reshape(25, 8, 128).reshape(200, 128)

    def put(p, value):
        ps[8 * p : 8 * p + 8, :] = value

    def get(p):
        return ps[8 * p : 8 * p + 8, :]

    def depth(n):
        return get(AT_DEPTH + n)

    for k in range(4):
        operate(u.at[k], u.at[k + 1], depth)
    for v in range(3):
        for n in range(25):
            terms = [u[k, 25 * v + n] for k in range(5)]
            put(25 * v + n, terms[0] + weighted(terms[1:], HALF))
            cb[25 * v + n] = terms[0] + weighted(terms[1:], WHOLE)
            if n in PLACE:
                first = weighted(terms[:4], HALF)
                tr1[16 * v + PLACE[n]] = first
                tr2[16 * v + PLACE[n]] = weighted(terms[:4], WHOLE) - first
    for f in range(4):
        sign = -1.0 if f % 2 == 0 else 1.0
        normal, tangent = (1, 2) if f < 2 else (2, 1)
        echo = jnp.where(walls[f], -2.0, 0.0)
        for k in range(5):
            n, opposite = FACES[f][k], FACES[f ^ 1][k]
            a = [tr1[16 * v + PLACE[n]] for v in range(3)]
            b = [grid.across(tr1[16 * v + PLACE[opposite]], f) for v in range(3)]
            for v in range(3):
                nf[15 * f + 5 * v + k] = b[v]
            own = depth(n)
            other = jnp.where(inner[f], grid.across(depth(opposite), f), own)
            speed = jnp.sqrt(jnp.maximum(own, other))
            cc[5 * f + k] = speed
            js = jnp.where(inner[f], b[0] - a[0], 0.0)
            jn = jnp.where(inner[f], b[normal] - a[normal], echo * a[normal])
            jt = jnp.where(inner[f], b[tangent] - a[tangent], 0.0)
            out = flux(js, jn, jt, speed, own, sign)
            for v, part in ((0, out[0]), (normal, out[1]), (tangent, out[2])):
                put(25 * v + n, get(25 * v + n) + part)
    put(AT_FLAG, jnp.where(cl[...] == 0, 1.0, 0.0))
    for v in range(3):
        for k in range(5):
            i = 5 * v + k
            for src, x, y in ((tr1, AT_X, AT_Y), (tr2, AT_X2, AT_Y2)):
                at = [src[16 * v + PLACE[FACES[f][k]]] for f in range(4)]
                put(x + i, jnp.where(grid.west, at[0], at[1]))
                put(y + i, jnp.where(grid.south, at[2], at[3]))
    blank = jnp.zeros((8, 128), F32)
    west, east, south, north = ([blank] * 5 for _ in range(4))
    for i in VALUES:
        a, by = divmod(i, 32)
        turned = lanes(get(i), by)
        west[a] = jnp.where(col == by, turned, west[a])
        east[a] = jnp.where(col == (31 + by) % 32, turned, east[a])
    east = [lanes(x, -31) for x in east]
    for group in range(IN_ALL // 8):
        a, g = divmod(group, 4)
        base = group
        if group >= 13:
            base = {13: 17, 14: 18, 15: 19, 16: 20, 17: 13, 18: 14}[group]
        here = lane // 32 == g
        low = ps[pl.ds(64 * base, 8, stride=8), :]
        high = ps[pl.ds(64 * base + 7, 8, stride=8), :]
        south[a] = jnp.where(here, lanes(low, 32 * g), south[a])
        north[a] = jnp.where(here, lanes(high, 32 * g + 32), north[a])
    for slot, out in enumerate((ex, eo, es)):
        for a in range(5):
            out[a] = jnp.where(
                slots[0] == slot,
                west[a],
                jnp.where(slots[1] == slot, east[a], jnp.where(slots[2] == slot, south[a], north[a])),
            )
    corner = ((col == 0) | (col == 31)) & (((sub == 0) & (lane < 32)) | ((sub == 7) & (lane >= 96)))
    for which, at, low, high, mask in ((0, AT_Y, 2, 3, grid.south), (1, AT_X, 0, 1, grid.west)):
        total = blank
        for i in range(20):
            value = get(at + i) if i < 15 else jnp.where(mask, depth(FACES[low][i - 15]), depth(FACES[high][i - 15]))
            total = total + lanes(jnp.where(corner, value, 0.0), i)
        dg[which] = total


def second_kernel(
    rx, ro, rs, dx, do, ps, cb, tr1, tr2, nf, cc, near_in, owner_in, upd, se, so, hs, m, g, late, near, owner
):
    grid = Grid()
    lane, sub, col = grid.lane, grid.sub, grid.col
    spread_ints(near_in, near)
    spread_ints(owner_in, owner)
    walls, remotes, slots = face_facts(near, owner)

    def get(p):
        return ps[8 * p : 8 * p + 8, :]

    def depth(n):
        return get(AT_DEPTH + n)

    def halo(p):
        return hs[8 * p : 8 * p + 8, :]

    def halo_depth(n):
        return halo(AT_DEPTH + n)

    is_w, is_e = col == 0, col == 16
    is_x = is_w | is_e
    is_s, is_n = (sub == 0) & ~is_x, (sub == 7) & ~is_x

    def place(x, base):
        return jnp.where(lane < 16, lanes(x, 1 + base), jnp.where(lane < 32, lanes(x, 2 + base), lanes(x, 3 + base)))

    def to_halo(x, y):
        x = jnp.where(is_w, x, lanes(x, -15))
        y = place(jnp.where(sub == 7, lanes(y, 32), y), 0)
        return jnp.where(is_x, x, y)

    def from_halo(v):
        x = jnp.where(is_w, v, lanes(v, 15))
        y = jnp.where(lane < 15, lanes(v, -1), jnp.where(lane < 30, lanes(v, -2), lanes(v, -3)))
        return x, jnp.where(sub == 7, lanes(y, 96), y)

    def facing(at):
        return lambda k: jnp.where(
            is_w, at(FACES[1][k]), jnp.where(is_e, at(FACES[0][k]), jnp.where(is_s, at(FACES[3][k]), at(FACES[2][k])))
        )

    got = [
        [jnp.where(slots[f] == 0, rx[a], jnp.where(slots[f] == 1, ro[a], rs[a])) for a in range(5)] for f in range(4)
    ]
    for group in range(IN_ALL // 8):
        a, q = divmod(group, 4)
        hs[pl.ds(64 * group, 8, stride=8), :] = place(got[2][a], -32 * q)
        hs[pl.ds(64 * group + 7, 8, stride=8), :] = place(got[3][a], -32 * q)
    mixed = []
    for a in range(5):
        mixed.append(jnp.where(grid.west, got[0][a], lanes(got[1][a], 16)))
        mixed.append(jnp.where(grid.west, lanes(got[0][a], -16), got[1][a]))
    for i in VALUES:
        a, by = divmod(i, 16)
        hs[8 * i : 8 * i + 8, :] = jnp.where(is_x, lanes(mixed[a], -by), halo(i))

    for i in range(75):
        g[0, i] = halo(i)

    def raise_at(node, mask, parts):
        for v in range(3):
            g[0, 25 * v + node] = g[0, 25 * v + node] + jnp.where(mask, parts[v], 0.0)

    def jump_parts(a, b, along_x, speed, own, sign):
        j = [b[v] - a[v] for v in range(3)]
        cs, cn, ct = flux(
            j[0], jnp.where(along_x, j[1], j[2]), jnp.where(along_x, j[2], j[1]), speed, own, sign
        )
        return cs, jnp.where(along_x, cn, ct), jnp.where(along_x, ct, cn)

    inward = jnp.where(is_w | is_s, 1.0, -1.0)
    speeds = []
    for k in range(5):
        a = [halo(IN_FACE + 5 * v + k) for v in range(3)]
        b = [to_halo(get(AT_X + 5 * v + k), get(AT_Y + 5 * v + k)) for v in range(3)]
        own = facing(halo_depth)(k)
        other = to_halo(
            jnp.where(grid.west, depth(FACES[0][k]), depth(FACES[1][k])),
            jnp.where(grid.south, depth(FACES[2][k]), depth(FACES[3][k])),
        )
        speed = jnp.sqrt(jnp.maximum(own, other))
        speeds.append(speed)
        parts = jump_parts(a, b, is_x, speed, own, inward)
        for mask, face in ((is_w, 1), (is_e, 0), (is_s, 3), (is_n, 2)):
            raise_at(FACES[face][k], mask, parts)

    def diagonal(f, h, which):
        slot = jnp.where(slots[f] == 2, slots[h], slots[f])
        return jnp.where(slot == 0, dx[which], do[which])

    there = [[(slots[f] < 3) & (slots[h] < 3) for h in (2, 3)] for f in (0, 1)]

    def shifted(x, by, down):
        return subs(lanes(x, by), down)

    low = sub == 0
    side_w = jnp.where(low, shifted(diagonal(0, 2, 0), 1, 1), shifted(diagonal(0, 3, 0), 65, -1))
    side_e = jnp.where(low, shifted(diagonal(1, 2, 0), 48, 1), shifted(diagonal(1, 3, 0), 112, -1))
    side_y = jnp.where(
        lane < 30,
        jnp.where(low, shifted(diagonal(0, 2, 1), 2, 1), shifted(diagonal(0, 3, 1), 98, -1)),
        jnp.where(low, shifted(diagonal(1, 2, 1), 66, 1), shifted(diagonal(1, 3, 1), 34, -1)),
    )

    def beyond(i):
        return jnp.where(is_w, lanes(side_w, -i), jnp.where(is_e, lanes(side_e, -i), lanes(side_y, -i)))

    low, high = sub == 0, sub == 7
    at_s = low & (((lane == 0) & there[0][0]) | ((lane == 16) & there[1][0]))
    at_n = high & (((lane == 96) & there[0][1]) | ((lane == 112) & there[1][1]))
    at_w = (lane == 1) & ((low & there[0][0]) | (high & there[0][1]))
    at_e = (lane == 34) & ((low & there[1][0]) | (high & there[1][1]))
    outward = jnp.where(at_n | at_e, 1.0, -1.0)
    for k in range(5):
        a = [halo(IN_SIDE + 5 * v + k) for v in range(3)]
        b = [beyond(5 * v + k) for v in range(3)]
        own = jnp.where(
            at_s,
            halo_depth(FACES[2][k]),
            jnp.where(at_n, halo_depth(FACES[3][k]), jnp.where(at_w, halo_depth(FACES[0][k]), halo_depth(FACES[1][k]))),
        )
        speed = jnp.sqrt(jnp.maximum(own, beyond(15 + k)))
        parts = jump_parts(a, b, ~is_x, speed, own, outward)
        for mask, face in ((at_w, 0), (at_e, 1), (at_s, 2), (at_n, 3)):
            raise_at(FACES[face][k], mask, parts)

    for i in range(75):
        m[0, i] = get(i)
    for k in range(5):
        speed_x, speed_y = from_halo(speeds[k])
        sent = [from_halo(halo(IN_FACE + 5 * v + k)) for v in range(3)]
        for axis, speed, at in ((0, speed_x, AT_X), (1, speed_y, AT_Y)):
            first, last = 2 * axis, 2 * axis + 1
            side = grid.south if axis else grid.west
            normal, tangent = (2, 1) if axis else (1, 2)
            j = [sent[v][axis] - get(at + 5 * v + k) for v in range(3)]
            own = jnp.where(side, depth(FACES[first][k]), depth(FACES[last][k]))
            out = flux(j[0], j[normal], j[tangent], speed, own, jnp.where(side, -1.0, 1.0))
            for f in (first, last):
                n = FACES[f][k]
                for v, part in ((0, out[0]), (normal, out[1]), (tangent, out[2])):
                    m[0, 25 * v + n] = m[0, 25 * v + n] + jnp.where(remotes[f], part, 0.0)

    for k in range(4):
        operate(m.at[k], m.at[k + 1], depth)
    for k in range(3):
        operate(g.at[k], g.at[k + 1], halo_depth)
    fine = get(AT_FLAG) > 0.5
    halo_fine = halo(AT_FLAG) > 0.5
    halo_late = []
    for v in range(3):
        for k in range(5):
            value = facing(lambda n: weighted([g[q, 25 * v + n] for q in range(4)], HALF))(k)
            halo_late.append(from_halo(jnp.where(halo_fine, value, halo(IN_SECOND + 5 * v + k))))
    for v in range(3):
        for n in range(25):
            terms = [m[k, 25 * v + n] for k in range(5)]
            upd[25 * v + n] = jnp.where(fine, terms[0] + weighted(terms[1:], HALF), cb[25 * v + n])
            if n in PLACE:
                late[16 * v + PLACE[n]] = weighted(terms[:4], HALF)
    for f in range(4):
        sign = -1.0 if f % 2 == 0 else 1.0
        axis = f // 2
        normal, tangent = (2, 1) if axis else (1, 2)
        for k in range(5):
            n, opposite = FACES[f][k], FACES[f ^ 1][k]
            speed_out = from_halo(speeds[k])[axis]
            speed = jnp.where(remotes[f], speed_out, cc[5 * f + k])
            j, a_list = [], []
            for v in range(3):
                at, across = 16 * v + PLACE[n], 16 * v + PLACE[opposite]
                a = jnp.where(fine, late[at], tr1[at] + tr2[at])
                sent = grid.across(jnp.where(fine, late[across], tr2[across]), f)
                sent = jnp.where(remotes[f], halo_late[5 * v + k][axis], sent)
                before = jnp.where(remotes[f], from_halo(halo(IN_FACE + 5 * v + k))[axis], nf[15 * f + 5 * v + k])
                b = jnp.where(fine, sent, before + sent)
                a_list.append(a)
                j.append(b - a)
            js = jnp.where(walls[f], 0.0, j[0])
            jn = jnp.where(walls[f], -2.0 * a_list[normal], j[normal])
            jt = jnp.where(walls[f], 0.0, j[tangent])
            out = flux(js, jn, jt, speed, depth(n), sign)
            for v, part in ((0, out[0]), (normal, out[1]), (tangent, out[2])):
                upd[25 * v + n] = upd[25 * v + n] + part
    even = (lane // 32) % 2 == 0
    for p in range(38):
        one = upd[2 * p]
        two = upd[min(2 * p + 1, 74)]
        se[p] = jnp.where(even, one, lanes(two, 32))
        so[p] = jnp.where(even, lanes(two, -32), one)


def third_kernel(swap, re, ro, upd, out, buf):
    grid = Grid()
    group = grid.lane // 32
    even = group % 2 == 0
    row = grid.sub * 4 + group
    moves = jnp.zeros((8, 128), jnp.int32)
    for b in range(32):
        moves = jnp.where(row == b, swap[b], moves)
    moves = moves > 0
    for i in range(75):
        e, o = re[i // 2], ro[i // 2]
        if i % 2:
            e, o = lanes(e, -32), lanes(o, 32)
        buf[i] = jnp.where(moves, jnp.where(even, e, o), upd[i])
    out[...] = buf[...].reshape(3, 25, 1024)


VM = pl.BlockSpec(memory_space=pltpu.VMEM)
PARAMS = pltpu.CompilerParams(vmem_limit_bytes=40 * 1024 * 1024)


def planes(*counts):
    return [jax.ShapeDtypeStruct((c, 8, 128), F32) for c in counts]


def local(sea_state, water_depth, neighbours, neighbour_owner, clusters, block_swap):
    devices = lax.axis_size("curve")
    odd_swap = [(i, i + 1) for i in range(1, devices - 1, 2)] + [(i + 1, i) for i in range(1, devices - 1, 2)]
    chip_swap = [(i, i ^ 1) for i in range(devices)]
    far = devices // 2

    def passed(x, pairs):
        return lax.ppermute(x, "curve", pairs)

    ex, eo, es, dg, ps, cb, tr1, tr2, nf, cc = pl.pallas_call(
        first_kernel,
        out_shape=planes(5, 5, 5, 2) + [jax.ShapeDtypeStruct((8 * PLANES, 128), F32)] + planes(75, 48, 48, 60, 20),
        in_specs=[VM] * 5,
        out_specs=[VM] * 10,
        scratch_shapes=[pltpu.VMEM((5, 75, 8, 128), F32)] + [pltpu.VMEM((4, 8, 128), jnp.int32)] * 2,
        compiler_params=PARAMS,
        name="predict",
    )(sea_state, water_depth, neighbours, neighbour_owner, clusters.reshape(8, 128))
    ro = passed(eo, odd_swap)
    do = passed(dg, [(i, (j + far) % devices) for i, j in odd_swap])
    dx = passed(dg, [(i, (j + far) % devices) for i, j in chip_swap])
    rs = passed(es, [(i, (i + far) % devices) for i in range(devices)])
    rx = passed(ex, chip_swap)
    upd, se, so = pl.pallas_call(
        second_kernel,
        out_shape=planes(75, 38, 38),
        in_specs=[VM] * 13,
        out_specs=[VM] * 3,
        scratch_shapes=[
            pltpu.VMEM((8 * 160, 128), F32),
            pltpu.VMEM((5, 75, 8, 128), F32),
            pltpu.VMEM((4, 75, 8, 128), F32),
            pltpu.VMEM((48, 8, 128), F32),
        ]
        + [pltpu.VMEM((4, 8, 128), jnp.int32)] * 2,
        compiler_params=PARAMS,
        name="correct",
    )(rx, ro, rs, dx, do, ps, cb, tr1, tr2, nf, cc, neighbours, neighbour_owner)
    got_odd = passed(so, odd_swap)
    got_even = passed(se, chip_swap)
    return pl.pallas_call(
        third_kernel,
        out_shape=jax.ShapeDtypeStruct((3, 25, 1024), F32),
        in_specs=[pl.BlockSpec(memory_space=pltpu.SMEM)] + [VM] * 3,
        out_specs=VM,
        scratch_shapes=[pltpu.VMEM((75, 8, 128), F32)],
        compiler_params=PARAMS,
        name="migrate",
    )(block_swap, got_even, got_odd, upd)


def solution(mesh):
    return jax.shard_map(
        local,
        mesh=mesh,
        in_specs=(
            P(None, None, "curve"),
            P(None, "curve"),
            P(None, "curve"),
            P(None, "curve"),
            P("curve"),
            P("curve"),
        ),
        out_specs=P(None, None, "curve"),
        check_vma=False,
    )
```

```python
import math

import jax
import jax.numpy as jnp
import numpy as np
from jax import lax
from jax.experimental import pallas as pl
from jax.experimental.pallas import tpu as pltpu
from jax.sharding import PartitionSpec as P

F32 = jnp.float32
FACES = ((0, 5, 10, 15, 20), (4, 9, 14, 19, 24), (0, 1, 2, 3, 4), (20, 21, 22, 23, 24))
EDGE = tuple(sorted({n for face in FACES for n in face}))
PLACE = {n: i for i, n in enumerate(EDGE)}
LIFT = 0.06 * 10.0 * 0.5
HALF = [0.5 ** (k + 1) / math.factorial(k + 1) for k in range(4)]
WHOLE = [1.0 / math.factorial(k + 1) for k in range(4)]
AT_DEPTH, AT_FLAG, AT_X, AT_X2, AT_Y, AT_Y2, PLANES = 75, 100, 104, 120, 136, 152, 168
IN_FACE, IN_SECOND, IN_SIDE, IN_ALL = 104, 120, 136, 152
VALUES = [i for i in range(IN_ALL) if i < 101 or (i >= 104 and (i - 104) % 16 < 15)]


def derivative_matrix():
    points = np.array([-1.0, -np.sqrt(3.0 / 7.0), 0.0, np.sqrt(3.0 / 7.0), 1.0])
    gaps = points[:, None] - points[None, :] + np.eye(5)
    weights = 1.0 / gaps.prod(axis=1)
    matrix = weights[None, :] / weights[:, None] / gaps
    matrix -= np.diag(np.diag(matrix))
    return matrix - np.diag(matrix.sum(axis=1))


STEP = -0.06 * derivative_matrix()


def slope(f):
    even_a, even_b, odd_a, odd_b = f[0] + f[4], f[1] + f[3], f[0] - f[4], f[1] - f[3]
    twice = f[2] + f[2]
    even_a, even_b = even_a - twice, even_b - twice
    out = [None] * 5
    for i in (0, 1):
        minus = float(STEP[i, 0] + STEP[i, 4]) * 0.5 * even_a + float(STEP[i, 1] + STEP[i, 3]) * 0.5 * even_b
        plus = float(STEP[i, 0] - STEP[i, 4]) * 0.5 * odd_a + float(STEP[i, 1] - STEP[i, 3]) * 0.5 * odd_b
        out[i], out[4 - i] = plus + minus, plus - minus
    out[2] = float(STEP[2, 0]) * odd_a + float(STEP[2, 1]) * odd_b
    return out


def operate(src, dst, depth):
    spread = [None] * 25
    for j in range(5):
        line = [5 * j + i for i in range(5)]
        grad = slope([src[n] for n in line])
        part = slope([src[25 + n] for n in line])
        for i, n in enumerate(line):
            dst[25 + n] = depth(n) * grad[i]
            dst[n] = part[i]
    for i in range(5):
        line = [5 * j + i for j in range(5)]
        grad = slope([src[n] for n in line])
        part = slope([src[50 + n] for n in line])
        for j, n in enumerate(line):
            dst[50 + n] = depth(n) * grad[j]
            dst[n] = dst[n] + part[j]


def weighted(values, weights):
    total = weights[0] * values[0]
    for value, weight in zip(values[1:], weights[1:]):
        total = total + weight * value
    return total


def lanes(x, by):
    return x if by % 128 == 0 else pltpu.roll(x, by % 128, 1)


def subs(x, by):
    return pltpu.roll(x, by % 8, 0)


class Grid:
    def __init__(self):
        self.lane = lax.broadcasted_iota(jnp.int32, (8, 128), 1)
        self.sub = lax.broadcasted_iota(jnp.int32, (8, 128), 0)
        self.col = self.lane % 32
        self.west = self.col < 16
        self.south = self.sub < 4

    def across(self, x, face):
        if face == 0:
            return lanes(x, 1)
        if face == 1:
            return lanes(x, -1)
        if face == 2:
            y = lanes(x, 32)
            return jnp.where(self.lane < 32, subs(y, 1), y)
        y = lanes(x, -32)
        return jnp.where(self.lane >= 96, subs(y, -1), y)


def spread_ints(ref, out):
    for j in range(8):
        out[:, j, :] = ref[:, 128 * j : 128 * j + 128]


def face_facts(near, owner):
    me = lax.axis_index("curve")
    odd = me % 2
    chip = me + 1 - 2 * odd
    swap = me - 1 + 2 * odd
    walls, remotes, slots = [], [], []
    for f in range(4):
        wall = near[f] < 0
        remote = (near[f] >= 0) & (owner[f] != me)
        peer = jnp.max(jnp.where(remote, owner[f], -1).astype(F32)).astype(jnp.int32)
        walls.append(wall)
        remotes.append(remote)
        slot = jnp.where(peer == chip, 0, jnp.where(peer == swap, 1, 2))
        slots.append(jnp.where(peer < 0, 3, slot))
    return walls, remotes, slots


def flux(js, jn, jt, speed, depth, sign):
    lifted = LIFT * speed
    turn = LIFT * sign
    return lifted * js - turn * jn, lifted * jn - depth * (turn * js), lifted * jt


def first_kernel(
    sea_in, dep_in, near_in, owner_in, cl_in, ex, eo, es, ps, cb, tr1, tr2, nf, cc, near, owner, u, sea, dep, nb, ow, cl, sems
):
    copies = [
        pltpu.make_async_copy(src, dst, sems.at[i])
        for i, (src, dst) in enumerate(((sea_in, sea), (dep_in, dep), (near_in, nb), (owner_in, ow), (cl_in, cl)))
    ]
    for copy in copies:
        copy.start()
    grid = Grid()
    lane, sub, col = grid.lane, grid.sub, grid.col
    for copy in copies:
        copy.wait()
    spread_ints(nb, near)
    spread_ints(ow, owner)
    walls, remotes, slots = face_facts(near, owner)
    inner = [~(walls[f] | remotes[f]) for f in range(4)]
    u[0] = sea[...].reshape(75, 8, 128)
    ps[8 * AT_DEPTH : 8 * AT_FLAG, :] = dep[...].reshape(25, 8, 128).reshape(200, 128)

    def put(p, value):
        ps[8 * p : 8 * p + 8, :] = value

    def get(p):
        return ps[8 * p : 8 * p + 8, :]

    def depth(n):
        return get(AT_DEPTH + n)

    for k in range(4):
        operate(u.at[k], u.at[k + 1], depth)
    for v in range(3):
        for n in range(25):
            terms = [u[k, 25 * v + n] for k in range(5)]
            put(25 * v + n, terms[0] + weighted(terms[1:], HALF))
            cb[25 * v + n] = terms[0] + weighted(terms[1:], WHOLE)
            if n in PLACE:
                first = weighted(terms[:4], HALF)
                tr1[16 * v + PLACE[n]] = first
                tr2[16 * v + PLACE[n]] = weighted(terms[:4], WHOLE) - first
    for f in range(4):
        sign = -1.0 if f % 2 == 0 else 1.0
        normal, tangent = (1, 2) if f < 2 else (2, 1)
        echo = jnp.where(walls[f], -2.0, 0.0)
        for k in range(5):
            n, opposite = FACES[f][k], FACES[f ^ 1][k]
            a = [tr1[16 * v + PLACE[n]] for v in range(3)]
            b = [grid.across(tr1[16 * v + PLACE[opposite]], f) for v in range(3)]
            for v in range(3):
                nf[15 * f + 5 * v + k] = b[v]
            own = depth(n)
            other = jnp.where(inner[f], grid.across(depth(opposite), f), own)
            speed = jnp.sqrt(jnp.maximum(own, other))
            cc[5 * f + k] = speed
            js = jnp.where(inner[f], b[0] - a[0], 0.0)
            jn = jnp.where(inner[f], b[normal] - a[normal], echo * a[normal])
            jt = jnp.where(inner[f], b[tangent] - a[tangent], 0.0)
            out = flux(js, jn, jt, speed, own, sign)
            for v, part in ((0, out[0]), (normal, out[1]), (tangent, out[2])):
                put(25 * v + n, get(25 * v + n) + part)
    put(AT_FLAG, jnp.where(cl[...] == 0, 1.0, 0.0))
    for v in range(3):
        for k in range(5):
            i = 5 * v + k
            for src, x, y in ((tr1, AT_X, AT_Y), (tr2, AT_X2, AT_Y2)):
                at = [src[16 * v + PLACE[FACES[f][k]]] for f in range(4)]
                put(x + i, jnp.where(grid.west, at[0], at[1]))
                put(y + i, jnp.where(grid.south, at[2], at[3]))
    blank = jnp.zeros((8, 128), F32)
    west, east, south, north = ([blank] * 5 for _ in range(4))
    for i in VALUES:
        a, by = divmod(i, 32)
        by = 2 * by if by < 16 else 2 * by - 31
        turned = lanes(get(i), by)
        west[a] = jnp.where(col == by, turned, west[a])
        east[a] = jnp.where(col == (31 + by) % 32, turned, east[a])
    east = [lanes(x, -31) for x in east]
    for group in range(IN_ALL // 8):
        a, g = divmod(group, 4)
        base = group
        if group >= 13:
            base = {13: 17, 14: 18, 15: 19, 16: 20, 17: 13, 18: 14}[group]
        here = lane // 32 == g
        low = ps[pl.ds(64 * base, 8, stride=8), :]
        high = ps[pl.ds(64 * base + 7, 8, stride=8), :]
        south[a] = jnp.where(here, lanes(low, 32 * g), south[a])
        north[a] = jnp.where(here, lanes(high, 32 * g + 32), north[a])
    for slot, out in enumerate((ex, eo, es)):
        for a in range(5):
            out[a] = jnp.where(
                slots[0] == slot,
                west[a],
                jnp.where(slots[1] == slot, east[a], jnp.where(slots[2] == slot, south[a], north[a])),
            )
    corner = ((col == 0) | (col == 31)) & (((sub == 0) & (lane < 32)) | ((sub == 7) & (lane >= 96)))
    for which, at, low, high, mask in ((0, AT_Y, 2, 3, grid.south), (1, AT_X, 0, 1, grid.west)):
        total = blank
        for i in range(20):
            value = get(at + i) if i < 15 else jnp.where(mask, depth(FACES[low][i - 15]), depth(FACES[high][i - 15]))
            total = total + lanes(jnp.where(corner, value, 0.0), i)
        es[5 + which] = total


def second_kernel(
    rx, ro, rs, ps, cb, tr1, tr2, nf, cc, near, owner, upd, se, so, hx, hy, m, gx, gy, late, before, after, fast
):
    grid = Grid()
    lane, sub = grid.lane, grid.sub
    walls, remotes, slots = face_facts(near, owner)

    def get(p):
        return ps[8 * p : 8 * p + 8, :]

    def depth(n):
        return get(AT_DEPTH + n)

    got = [
        [jnp.where(slots[f] == 0, rx[a], jnp.where(slots[f] == 1, ro[a], rs[a])) for a in range(5)] for f in range(4)
    ]
    for a in range(5):
        pair = (
            jnp.where(lane % 2 == 0, got[0][a], lanes(got[1][a], 31)),
            jnp.where(lane % 2 == 0, lanes(got[0][a], -1), lanes(got[1][a], 30)),
        )
        for i in VALUES:
            if i // 32 == a:
                hx[8 * i : 8 * i + 8, :] = lanes(pair[i % 32 // 16], -2 * (i % 16))
    for group in range(IN_ALL // 8):
        a, q = divmod(group, 4)
        hy[pl.ds(64 * group, 8, stride=8), :] = lanes(got[2][a], -32 * q)
        hy[pl.ds(64 * group + 7, 8, stride=8), :] = lanes(got[3][a], 96 - 32 * q)

    def diagonal(f, h, which):
        slot = jnp.where(slots[f] == 2, slots[h], slots[f])
        return jnp.where(slot == 0, rx[5 + which], ro[5 + which])

    there = [[(slots[f] < 3) & (slots[h] < 3) for h in (2, 3)] for f in (0, 1)]
    low, high = sub == 0, sub == 7
    corners = []
    for which in (0, 1):
        corners.append(
            jnp.where(
                grid.south,
                subs(jnp.where(lane < 25, lanes(diagonal(0, 2, which), 1), lanes(diagonal(1, 2, which), 63)), 1),
                subs(
                    jnp.where(
                        (lane >= 96) & (lane < 120), lanes(diagonal(0, 3, which), 65), lanes(diagonal(1, 3, which), 127)
                    ),
                    -1,
                ),
            )
        )
    corner_w = (low & (lane == 0) & there[0][0]) | (high & (lane == 96) & there[0][1])
    corner_e = (low & (lane == 31) & there[1][0]) | (high & (lane == 127) & there[1][1])
    corner_s = low & (corner_w | corner_e)
    corner_n = high & (corner_w | corner_e)

    for i in range(75):
        m[0, i] = get(i)
    for axis, h, g, side, at in ((0, hx, gx, grid.west, AT_X), (1, hy, gy, grid.south, AT_Y)):
        first, last = 2 * axis, 2 * axis + 1
        normal, tangent = (2, 1) if axis else (1, 2)
        sign = jnp.where(side, 1.0, -1.0)

        def halo(p, h=h):
            return h[8 * p : 8 * p + 8, :]

        def halo_depth(n, halo=halo):
            return halo(AT_DEPTH + n)

        for i in range(75):
            g[0, i] = halo(i)
        for k in range(5):
            n, opposite = FACES[first][k], FACES[last][k]
            a = [halo(IN_FACE + 5 * v + k) for v in range(3)]
            b = [get(at + 5 * v + k) for v in range(3)]
            own = jnp.where(side, depth(n), depth(opposite))
            other = jnp.where(side, halo_depth(opposite), halo_depth(n))
            speed = jnp.sqrt(jnp.maximum(own, other))
            j = [b[v] - a[v] for v in range(3)]
            out = flux(j[0], j[normal], j[tangent], speed, other, sign)
            for v, part in ((0, out[0]), (normal, out[1]), (tangent, out[2])):
                g[0, 25 * v + opposite] = g[0, 25 * v + opposite] + jnp.where(side, part, 0.0)
                g[0, 25 * v + n] = g[0, 25 * v + n] + jnp.where(side, 0.0, part)
            out = flux(-j[0], -j[normal], -j[tangent], speed, own, -sign)
            for f in (first, last):
                node = FACES[f][k]
                fast[5 * f + k] = jnp.where(remotes[f], speed, cc[5 * f + k])
                for v in range(3):
                    before[15 * f + 5 * v + k] = jnp.where(remotes[f], a[v], nf[15 * f + 5 * v + k])
                for v, part in ((0, out[0]), (normal, out[1]), (tangent, out[2])):
                    m[0, 25 * v + node] = m[0, 25 * v + node] + jnp.where(remotes[f], part, 0.0)
        first, last = 2 - first, 3 - first
        on_first, on_last = (corner_w, corner_e) if axis else (corner_s, corner_n)
        side = grid.west if axis else grid.south
        sign = jnp.where(side, -1.0, 1.0)
        for k in range(5):
            a = [halo(IN_SIDE + 5 * v + k) for v in range(3)]
            b = [lanes(corners[axis], -(5 * v + k)) for v in range(3)]
            own = jnp.where(side, halo_depth(FACES[first][k]), halo_depth(FACES[last][k]))
            speed = jnp.sqrt(jnp.maximum(own, lanes(corners[axis], -(15 + k))))
            j = [b[v] - a[v] for v in range(3)]
            out = flux(j[0], j[tangent], j[normal], speed, own, sign)
            for v, part in ((0, out[0]), (tangent, out[1]), (normal, out[2])):
                for f, mask in ((first, on_first), (last, on_last)):
                    at_node = 25 * v + FACES[f][k]
                    g[0, at_node] = g[0, at_node] + jnp.where(mask, part, 0.0)
        for k in range(3):
            operate(g.at[k], g.at[k + 1], halo_depth)
        side = grid.south if axis else grid.west
        halo_fine = halo(AT_FLAG) > 0.5
        for v in range(3):
            for k in range(5):
                n, opposite = FACES[2 * axis][k], FACES[2 * axis + 1][k]
                terms = [jnp.where(side, g[q, 25 * v + opposite], g[q, 25 * v + n]) for q in range(4)]
                after[15 * axis + 5 * v + k] = jnp.where(
                    halo_fine, weighted(terms, HALF), halo(IN_SECOND + 5 * v + k)
                )

    for k in range(4):
        operate(m.at[k], m.at[k + 1], depth)
    fine = get(AT_FLAG) > 0.5
    for v in range(3):
        for n in range(25):
            terms = [m[k, 25 * v + n] for k in range(5)]
            upd[25 * v + n] = jnp.where(fine, terms[0] + weighted(terms[1:], HALF), cb[25 * v + n])
            if n in PLACE:
                late[16 * v + PLACE[n]] = weighted(terms[:4], HALF)
    for f in range(4):
        sign = -1.0 if f % 2 == 0 else 1.0
        axis = f // 2
        normal, tangent = (2, 1) if axis else (1, 2)
        for k in range(5):
            n, opposite = FACES[f][k], FACES[f ^ 1][k]
            speed = fast[5 * f + k]
            j, a_list = [], []
            for v in range(3):
                at, across = 16 * v + PLACE[n], 16 * v + PLACE[opposite]
                a = jnp.where(fine, late[at], tr1[at] + tr2[at])
                sent = grid.across(jnp.where(fine, late[across], tr2[across]), f)
                sent = jnp.where(remotes[f], after[15 * axis + 5 * v + k], sent)
                b = jnp.where(fine, sent, before[15 * f + 5 * v + k] + sent)
                a_list.append(a)
                j.append(b - a)
            js = jnp.where(walls[f], 0.0, j[0])
            jn = jnp.where(walls[f], -2.0 * a_list[normal], j[normal])
            jt = jnp.where(walls[f], 0.0, j[tangent])
            out = flux(js, jn, jt, speed, depth(n), sign)
            for v, part in ((0, out[0]), (normal, out[1]), (tangent, out[2])):
                upd[25 * v + n] = upd[25 * v + n] + part
    even = (lane // 32) % 2 == 0
    for p in range(38):
        one = upd[2 * p]
        two = upd[min(2 * p + 1, 74)]
        se[p] = jnp.where(even, one, lanes(two, 32))
        so[p] = jnp.where(even, lanes(two, -32), one)


def third_kernel(swap, re, ro, upd, out, buf):
    grid = Grid()
    group = grid.lane // 32
    even = group % 2 == 0
    row = grid.sub * 4 + group
    moves = jnp.zeros((8, 128), jnp.int32)
    for b in range(32):
        moves = jnp.where(row == b, swap[b], moves)
    moves = moves > 0
    for i in range(75):
        e, o = re[i // 2], ro[i // 2]
        if i % 2:
            e, o = lanes(e, -32), lanes(o, 32)
        buf[i] = jnp.where(moves, jnp.where(even, e, o), upd[i])
    out[...] = buf[...].reshape(3, 25, 1024)


VM = pl.BlockSpec(memory_space=pltpu.VMEM)
ANY = pl.BlockSpec(memory_space=pltpu.HBM)
PARAMS = pltpu.CompilerParams(vmem_limit_bytes=40 * 1024 * 1024)


def in_hbm(x):
    return pltpu.with_memory_space_constraint(x, pltpu.HBM)


def planes(*counts):
    return [jax.ShapeDtypeStruct((c, 8, 128), F32) for c in counts]


def local(sea_state, water_depth, neighbours, neighbour_owner, clusters, block_swap):
    devices = lax.axis_size("curve")
    odd_swap = [(i, i + 1) for i in range(1, devices - 1, 2)] + [(i + 1, i) for i in range(1, devices - 1, 2)]
    chip_swap = [(i, i ^ 1) for i in range(devices)]
    far = devices // 2

    def passed(x, pairs):
        return lax.ppermute(x, "curve", pairs)

    ex, eo, es, ps, cb, tr1, tr2, nf, cc, near, owner = pl.pallas_call(
        first_kernel,
        out_shape=planes(7, 7, 7)
        + [jax.ShapeDtypeStruct((8 * PLANES, 128), F32)]
        + planes(75, 48, 48, 60, 20)
        + [jax.ShapeDtypeStruct((4, 8, 128), jnp.int32)] * 2,
        in_specs=[ANY] * 5,
        out_specs=[VM] * 11,
        scratch_shapes=[
            pltpu.VMEM((5, 75, 8, 128), F32),
            pltpu.VMEM((3, 25, 1024), F32),
            pltpu.VMEM((25, 1024), F32),
            pltpu.VMEM((4, 1024), jnp.int32),
            pltpu.VMEM((4, 1024), jnp.int32),
            pltpu.VMEM((8, 128), jnp.int32),
            pltpu.SemaphoreType.DMA((5,)),
        ],
        compiler_params=PARAMS,
        name="predict",
    )(*(in_hbm(x) for x in (sea_state, water_depth, neighbours, neighbour_owner, clusters.reshape(8, 128))))
    rs = passed(es, [(i, (i + far) % devices) for i in range(devices)])
    ro = passed(lax.dynamic_update_slice(eo, rs[5:], (5, 0, 0)), odd_swap)
    rx = passed(lax.dynamic_update_slice(ex, rs[5:], (5, 0, 0)), chip_swap)
    upd, se, so = pl.pallas_call(
        second_kernel,
        out_shape=planes(75, 38, 38),
        in_specs=[VM] * 11,
        out_specs=[VM] * 3,
        scratch_shapes=[
            pltpu.VMEM((8 * 160, 128), F32),
            pltpu.VMEM((8 * 160, 128), F32),
            pltpu.VMEM((5, 75, 8, 128), F32),
            pltpu.VMEM((4, 75, 8, 128), F32),
            pltpu.VMEM((4, 75, 8, 128), F32),
            pltpu.VMEM((48, 8, 128), F32),
            pltpu.VMEM((60, 8, 128), F32),
            pltpu.VMEM((30, 8, 128), F32),
            pltpu.VMEM((20, 8, 128), F32),
        ],
        compiler_params=PARAMS,
        name="correct",
    )(rx, ro, rs, ps, cb, tr1, tr2, nf, cc, near, owner)
    got_odd = passed(so, odd_swap)
    got_even = passed(se, chip_swap)
    return pl.pallas_call(
        third_kernel,
        out_shape=jax.ShapeDtypeStruct((3, 25, 1024), F32),
        in_specs=[pl.BlockSpec(memory_space=pltpu.SMEM)] + [VM] * 3,
        out_specs=VM,
        scratch_shapes=[pltpu.VMEM((75, 8, 128), F32)],
        compiler_params=PARAMS,
        name="migrate",
    )(block_swap, got_even, got_odd, upd)


def solution(mesh):
    return jax.shard_map(
        local,
        mesh=mesh,
        in_specs=(
            P(None, None, "curve"),
            P(None, "curve"),
            P(None, "curve"),
            P(None, "curve"),
            P("curve"),
            P("curve"),
        ),
        out_specs=P(None, None, "curve"),
        check_vma=False,
    )
```

```python
import math

import jax
import jax.numpy as jnp
import numpy as np
from jax import lax
from jax.experimental import pallas as pl
from jax.experimental.pallas import tpu as pltpu
from jax.sharding import PartitionSpec as P

F32 = jnp.float32
FACES = ((0, 5, 10, 15, 20), (4, 9, 14, 19, 24), (0, 1, 2, 3, 4), (20, 21, 22, 23, 24))
EDGE = tuple(sorted({n for face in FACES for n in face}))
PLACE = {n: i for i, n in enumerate(EDGE)}
LIFT = 0.06 * 10.0 * 0.5
HALF = [0.5 ** (k + 1) / math.factorial(k + 1) for k in range(4)]
WHOLE = [1.0 / math.factorial(k + 1) for k in range(4)]
AT_DEPTH, AT_FLAG, AT_X, AT_X2, AT_Y, AT_Y2, PLANES = 75, 100, 104, 120, 136, 152, 168
IN_FACE, IN_SECOND, IN_SIDE, IN_ALL = 104, 120, 136, 152
VALUES = [i for i in range(IN_ALL) if i < 101 or (i >= 104 and (i - 104) % 16 < 15)]


def derivative_matrix():
    points = np.array([-1.0, -np.sqrt(3.0 / 7.0), 0.0, np.sqrt(3.0 / 7.0), 1.0])
    gaps = points[:, None] - points[None, :] + np.eye(5)
    weights = 1.0 / gaps.prod(axis=1)
    matrix = weights[None, :] / weights[:, None] / gaps
    matrix -= np.diag(np.diag(matrix))
    return matrix - np.diag(matrix.sum(axis=1))


STEP = -0.06 * derivative_matrix()


def slope(f):
    even_a, even_b, odd_a, odd_b = f[0] + f[4], f[1] + f[3], f[0] - f[4], f[1] - f[3]
    twice = f[2] + f[2]
    even_a, even_b = even_a - twice, even_b - twice
    out = [None] * 5
    for i in (0, 1):
        minus = float(STEP[i, 0] + STEP[i, 4]) * 0.5 * even_a + float(STEP[i, 1] + STEP[i, 3]) * 0.5 * even_b
        plus = float(STEP[i, 0] - STEP[i, 4]) * 0.5 * odd_a + float(STEP[i, 1] - STEP[i, 3]) * 0.5 * odd_b
        out[i], out[4 - i] = plus + minus, plus - minus
    out[2] = float(STEP[2, 0]) * odd_a + float(STEP[2, 1]) * odd_b
    return out


def operate(src, dst, depth):
    spread = [None] * 25
    for j in range(5):
        line = [5 * j + i for i in range(5)]
        grad = slope([src[n] for n in line])
        part = slope([src[25 + n] for n in line])
        for i, n in enumerate(line):
            dst[25 + n] = depth(n) * grad[i]
            dst[n] = part[i]
    for i in range(5):
        line = [5 * j + i for j in range(5)]
        grad = slope([src[n] for n in line])
        part = slope([src[50 + n] for n in line])
        for j, n in enumerate(line):
            dst[50 + n] = depth(n) * grad[j]
            dst[n] = dst[n] + part[j]


def weighted(values, weights):
    total = weights[0] * values[0]
    for value, weight in zip(values[1:], weights[1:]):
        total = total + weight * value
    return total


def lanes(x, by):
    return x if by % 128 == 0 else pltpu.roll(x, by % 128, 1)


def subs(x, by):
    return pltpu.roll(x, by % 8, 0)


class Grid:
    def __init__(self):
        self.lane = lax.broadcasted_iota(jnp.int32, (8, 128), 1)
        self.sub = lax.broadcasted_iota(jnp.int32, (8, 128), 0)
        self.col = self.lane % 32
        self.west = self.col < 16
        self.south = self.sub < 4

    def across(self, x, face):
        if face == 0:
            return lanes(x, 1)
        if face == 1:
            return lanes(x, -1)
        if face == 2:
            y = lanes(x, 32)
            return jnp.where(self.lane < 32, subs(y, 1), y)
        y = lanes(x, -32)
        return jnp.where(self.lane >= 96, subs(y, -1), y)


def spread_ints(ref, out):
    for j in range(8):
        out[:, j, :] = ref[:, 128 * j : 128 * j + 128]


def face_facts(near, owner, facts):
    me = lax.axis_index("curve")
    odd = me % 2
    chip = me + 1 - 2 * odd
    swap = me - 1 + 2 * odd
    for f in range(4):
        wall = near[f] < 0
        remote = (near[f] >= 0) & (owner[f] != me)
        peer = jnp.where(remote, owner[f], -1).astype(F32)
        peer = jnp.max(jnp.max(peer, axis=1, keepdims=True), axis=0, keepdims=True).astype(jnp.int32)
        peer = jnp.broadcast_to(peer, (8, 128))
        slot = jnp.where(peer == chip, 0, jnp.where(peer == swap, 1, 2))
        facts[f] = jnp.where(peer < 0, 3, slot)
        facts[4 + f] = jnp.where(wall, 1, jnp.where(remote, 2, 0))


def read_facts(facts):
    walls = [facts[4 + f] == 1 for f in range(4)]
    remotes = [facts[4 + f] == 2 for f in range(4)]
    return walls, remotes, [facts[f] for f in range(4)]


def flux(js, jn, jt, speed, depth, sign):
    lifted = LIFT * speed
    turn = LIFT * sign
    return lifted * js - turn * jn, lifted * jn - depth * (turn * js), lifted * jt


def side_edges(grid, get):
    blank = jnp.zeros((8, 128), F32)
    west, east = [blank] * 5, [blank] * 5
    for i in VALUES:
        a, by = divmod(i, 32)
        by = 2 * by if by < 16 else 2 * by - 31
        turned = lanes(get(i), by)
        west[a] = jnp.where(grid.col == by, turned, west[a])
        east[a] = jnp.where(grid.col == (31 + by) % 32, turned, east[a])
    return west, [lanes(x, -31) for x in east]


def row_edges(grid, ps):
    blank = jnp.zeros((8, 128), F32)
    south, north = [blank] * 5, [blank] * 5
    for group in range(IN_ALL // 8):
        a, g = divmod(group, 4)
        base = {13: 17, 14: 18, 15: 19, 16: 20, 17: 13, 18: 14}.get(group, group)
        here = grid.lane // 32 == g
        low = ps[pl.ds(64 * base, 8, stride=8), :]
        high = ps[pl.ds(64 * base + 7, 8, stride=8), :]
        south[a] = jnp.where(here, lanes(low, 32 * g), south[a])
        north[a] = jnp.where(here, lanes(high, 32 * g + 32), north[a])
    return south, north


def first_kernel(
    sea_in, dep_in, near_in, owner_in, cl_in, ex, eo, ps, u, tr1, tr2, nf, cc, facts, sea, dep, nb, ow, cl, near, owner, sems
):
    copies = [
        pltpu.make_async_copy(src, dst, sems.at[i])
        for i, (src, dst) in enumerate(((sea_in, sea), (dep_in, dep), (near_in, nb), (owner_in, ow), (cl_in, cl)))
    ]
    for copy in copies:
        copy.start()
    grid = Grid()
    lane, sub, col = grid.lane, grid.sub, grid.col
    for copy in copies:
        copy.wait()
    spread_ints(nb, near)
    spread_ints(ow, owner)
    face_facts(near, owner, facts)
    walls, remotes, slots = read_facts(facts)
    inner = [~(walls[f] | remotes[f]) for f in range(4)]
    u[0] = sea[...].reshape(75, 8, 128)
    ps[8 * AT_DEPTH : 8 * AT_FLAG, :] = dep[...].reshape(25, 8, 128).reshape(200, 128)

    def put(p, value):
        ps[8 * p : 8 * p + 8, :] = value

    def get(p):
        return ps[8 * p : 8 * p + 8, :]

    def depth(n):
        return get(AT_DEPTH + n)

    for k in range(4):
        operate(u.at[k], u.at[k + 1], depth)
    for v in range(3):
        for n in range(25):
            terms = [u[k, 25 * v + n] for k in range(5)]
            put(25 * v + n, terms[0] + weighted(terms[1:], HALF))
            if n in PLACE:
                first = weighted(terms[:4], HALF)
                tr1[16 * v + PLACE[n]] = first
                tr2[16 * v + PLACE[n]] = weighted(terms[:4], WHOLE) - first
    for f in range(4):
        sign = -1.0 if f % 2 == 0 else 1.0
        normal, tangent = (1, 2) if f < 2 else (2, 1)
        echo = jnp.where(walls[f], -2.0, 0.0)
        for k in range(5):
            n, opposite = FACES[f][k], FACES[f ^ 1][k]
            a = [tr1[16 * v + PLACE[n]] for v in range(3)]
            b = [grid.across(tr1[16 * v + PLACE[opposite]], f) for v in range(3)]
            for v in range(3):
                nf[15 * f + 5 * v + k] = b[v]
            own = depth(n)
            other = jnp.where(inner[f], grid.across(depth(opposite), f), own)
            speed = jnp.sqrt(jnp.maximum(own, other))
            cc[5 * f + k] = speed
            js = jnp.where(inner[f], b[0] - a[0], 0.0)
            jn = jnp.where(inner[f], b[normal] - a[normal], echo * a[normal])
            jt = jnp.where(inner[f], b[tangent] - a[tangent], 0.0)
            out = flux(js, jn, jt, speed, own, sign)
            for v, part in ((0, out[0]), (normal, out[1]), (tangent, out[2])):
                put(25 * v + n, get(25 * v + n) + part)
    put(AT_FLAG, jnp.where(cl[...] == 0, 1.0, 0.0))
    for v in range(3):
        for k in range(5):
            i = 5 * v + k
            for src, x, y in ((tr1, AT_X, AT_Y), (tr2, AT_X2, AT_Y2)):
                at = [src[16 * v + PLACE[FACES[f][k]]] for f in range(4)]
                put(x + i, jnp.where(grid.west, at[0], at[1]))
                put(y + i, jnp.where(grid.south, at[2], at[3]))
    west, east = side_edges(grid, get)
    for slot, out in ((0, ex), (1, eo)):
        for a in range(5):
            out[a] = jnp.where(slots[0] == slot, west[a], east[a])
    turned = jnp.max(jnp.where((slots[2] < 2) | (slots[3] < 2), 1.0, 0.0)) > 0.5

    @pl.when(turned)
    def _():
        south, north = row_edges(grid, ps)
        for slot, out in ((0, ex), (1, eo)):
            for a in range(5):
                out[a] = jnp.where(slots[2] == slot, south[a], jnp.where(slots[3] == slot, north[a], out[a]))

    blank = jnp.zeros((8, 128), F32)
    corner = ((col == 0) | (col == 31)) & (((sub == 0) & (lane < 32)) | ((sub == 7) & (lane >= 96)))
    for which, at, low, high, mask in ((0, AT_Y, 2, 3, grid.south), (1, AT_X, 0, 1, grid.west)):
        total = blank
        for i in range(20):
            value = get(at + i) if i < 15 else jnp.where(mask, depth(FACES[low][i - 15]), depth(FACES[high][i - 15]))
            total = total + lanes(jnp.where(corner, value, 0.0), i)
        ex[5 + which] = total
        eo[5 + which] = total


def messages_kernel(ps, u, facts, es, cb):
    grid = Grid()
    _, _, slots = read_facts(facts)
    south, north = row_edges(grid, ps)
    for a in range(5):
        es[a] = jnp.where(slots[2] == 2, south[a], north[a])
    for i in range(75):
        cb[i] = u[0, i] + weighted([u[k, i] for k in range(1, 5)], WHOLE)
    turned = jnp.max(jnp.where((slots[0] == 2) | (slots[1] == 2), 1.0, 0.0)) > 0.5

    @pl.when(turned)
    def _():
        west, east = side_edges(grid, lambda p: ps[8 * p : 8 * p + 8, :])
        for a in range(5):
            es[a] = jnp.where(slots[0] == 2, west[a], jnp.where(slots[1] == 2, east[a], es[a]))


def unpack_sides(grid, got, hx):
    for a in range(5):
        pair = (
            jnp.where(grid.lane % 2 == 0, got[0][a], lanes(got[1][a], 31)),
            jnp.where(grid.lane % 2 == 0, lanes(got[0][a], -1), lanes(got[1][a], 30)),
        )
        for i in VALUES:
            if i // 32 == a:
                hx[8 * i : 8 * i + 8, :] = lanes(pair[i % 32 // 16], -2 * (i % 16))


def sides_kernel(rx, ro, facts, hx):
    _, _, slots = read_facts(facts)
    unpack_sides(Grid(), [[jnp.where(slots[f] == 0, rx[a], ro[a]) for a in range(5)] for f in (0, 1)], hx)


def second_kernel(
    rx, ro, rs, ps, cb, tr1, tr2, nf, cc, facts, hx_in, upd, se, so, hx, hy, m, gx, gy, late, before, after, fast
):
    grid = Grid()
    lane, sub = grid.lane, grid.sub
    walls, remotes, slots = read_facts(facts)

    def get(p):
        return ps[8 * p : 8 * p + 8, :]

    def depth(n):
        return get(AT_DEPTH + n)

    got = [
        [jnp.where(slots[f] == 0, rx[a], jnp.where(slots[f] == 1, ro[a], rs[a])) for a in range(5)] for f in range(4)
    ]
    turned = jnp.max(jnp.where((slots[0] == 2) | (slots[1] == 2), 1.0, 0.0)) > 0.5

    @pl.when(turned)
    def _():
        unpack_sides(grid, got, hx)

    for group in range(IN_ALL // 8):
        a, q = divmod(group, 4)
        hy[pl.ds(64 * group, 8, stride=8), :] = lanes(got[2][a], -32 * q)
        hy[pl.ds(64 * group + 7, 8, stride=8), :] = lanes(got[3][a], 96 - 32 * q)

    def diagonal(f, h, which):
        slot = jnp.where(slots[f] == 2, slots[h], slots[f])
        return jnp.where(slot == 0, rs[5 + which], rs[7 + which])

    there = [[(slots[f] < 3) & (slots[h] < 3) for h in (2, 3)] for f in (0, 1)]
    low, high = sub == 0, sub == 7
    corners = []
    for which in (0, 1):
        corners.append(
            jnp.where(
                grid.south,
                subs(jnp.where(lane < 25, lanes(diagonal(0, 2, which), 1), lanes(diagonal(1, 2, which), 63)), 1),
                subs(
                    jnp.where(
                        (lane >= 96) & (lane < 120), lanes(diagonal(0, 3, which), 65), lanes(diagonal(1, 3, which), 127)
                    ),
                    -1,
                ),
            )
        )
    corner_w = (low & (lane == 0) & there[0][0]) | (high & (lane == 96) & there[0][1])
    corner_e = (low & (lane == 31) & there[1][0]) | (high & (lane == 127) & there[1][1])
    corner_s = low & (corner_w | corner_e)
    corner_n = high & (corner_w | corner_e)

    for i in range(75):
        m[0, i] = get(i)
    for axis, h, g, side, at in ((0, hx, gx, grid.west, AT_X), (1, hy, gy, grid.south, AT_Y)):
        first, last = 2 * axis, 2 * axis + 1
        normal, tangent = (2, 1) if axis else (1, 2)
        sign = jnp.where(side, 1.0, -1.0)

        def halo(p, h=h):
            return h[8 * p : 8 * p + 8, :]

        def halo_depth(n, halo=halo):
            return halo(AT_DEPTH + n)

        for i in range(75):
            g[0, i] = halo(i)
        for k in range(5):
            n, opposite = FACES[first][k], FACES[last][k]
            a = [halo(IN_FACE + 5 * v + k) for v in range(3)]
            b = [get(at + 5 * v + k) for v in range(3)]
            own = jnp.where(side, depth(n), depth(opposite))
            other = jnp.where(side, halo_depth(opposite), halo_depth(n))
            speed = jnp.sqrt(jnp.maximum(own, other))
            j = [b[v] - a[v] for v in range(3)]
            out = flux(j[0], j[normal], j[tangent], speed, other, sign)
            for v, part in ((0, out[0]), (normal, out[1]), (tangent, out[2])):
                g[0, 25 * v + opposite] = g[0, 25 * v + opposite] + jnp.where(side, part, 0.0)
                g[0, 25 * v + n] = g[0, 25 * v + n] + jnp.where(side, 0.0, part)
            out = flux(-j[0], -j[normal], -j[tangent], speed, own, -sign)
            for f in (first, last):
                node = FACES[f][k]
                fast[5 * f + k] = jnp.where(remotes[f], speed, cc[5 * f + k])
                for v in range(3):
                    before[15 * f + 5 * v + k] = jnp.where(remotes[f], a[v], nf[15 * f + 5 * v + k])
                for v, part in ((0, out[0]), (normal, out[1]), (tangent, out[2])):
                    m[0, 25 * v + node] = m[0, 25 * v + node] + jnp.where(remotes[f], part, 0.0)
        first, last = 2 - first, 3 - first
        on_first, on_last = (corner_w, corner_e) if axis else (corner_s, corner_n)
        side = grid.west if axis else grid.south
        sign = jnp.where(side, -1.0, 1.0)
        for k in range(5):
            a = [halo(IN_SIDE + 5 * v + k) for v in range(3)]
            b = [lanes(corners[axis], -(5 * v + k)) for v in range(3)]
            own = jnp.where(side, halo_depth(FACES[first][k]), halo_depth(FACES[last][k]))
            speed = jnp.sqrt(jnp.maximum(own, lanes(corners[axis], -(15 + k))))
            j = [b[v] - a[v] for v in range(3)]
            out = flux(j[0], j[tangent], j[normal], speed, own, sign)
            for v, part in ((0, out[0]), (tangent, out[1]), (normal, out[2])):
                for f, mask in ((first, on_first), (last, on_last)):
                    at_node = 25 * v + FACES[f][k]
                    g[0, at_node] = g[0, at_node] + jnp.where(mask, part, 0.0)
        for k in range(3):
            operate(g.at[k], g.at[k + 1], halo_depth)
        side = grid.south if axis else grid.west
        halo_fine = halo(AT_FLAG) > 0.5
        for v in range(3):
            for k in range(5):
                n, opposite = FACES[2 * axis][k], FACES[2 * axis + 1][k]
                terms = [jnp.where(side, g[q, 25 * v + opposite], g[q, 25 * v + n]) for q in range(4)]
                after[15 * axis + 5 * v + k] = jnp.where(
                    halo_fine, weighted(terms, HALF), halo(IN_SECOND + 5 * v + k)
                )

    for k in range(4):
        operate(m.at[k], m.at[k + 1], depth)
    fine = get(AT_FLAG) > 0.5
    for v in range(3):
        for n in range(25):
            terms = [m[k, 25 * v + n] for k in range(5)]
            upd[25 * v + n] = jnp.where(fine, terms[0] + weighted(terms[1:], HALF), cb[25 * v + n])
            if n in PLACE:
                late[16 * v + PLACE[n]] = weighted(terms[:4], HALF)
    for f in range(4):
        sign = -1.0 if f % 2 == 0 else 1.0
        axis = f // 2
        normal, tangent = (2, 1) if axis else (1, 2)
        for k in range(5):
            n, opposite = FACES[f][k], FACES[f ^ 1][k]
            speed = fast[5 * f + k]
            j, a_list = [], []
            for v in range(3):
                at, across = 16 * v + PLACE[n], 16 * v + PLACE[opposite]
                a = jnp.where(fine, late[at], tr1[at] + tr2[at])
                sent = grid.across(jnp.where(fine, late[across], tr2[across]), f)
                sent = jnp.where(remotes[f], after[15 * axis + 5 * v + k], sent)
                b = jnp.where(fine, sent, before[15 * f + 5 * v + k] + sent)
                a_list.append(a)
                j.append(b - a)
            js = jnp.where(walls[f], 0.0, j[0])
            jn = jnp.where(walls[f], -2.0 * a_list[normal], j[normal])
            jt = jnp.where(walls[f], 0.0, j[tangent])
            out = flux(js, jn, jt, speed, depth(n), sign)
            for v, part in ((0, out[0]), (normal, out[1]), (tangent, out[2])):
                upd[25 * v + n] = upd[25 * v + n] + part
    even = (lane // 32) % 2 == 0
    for p in range(38):
        one = upd[2 * p]
        two = upd[min(2 * p + 1, 74)]
        se[p] = jnp.where(even, one, lanes(two, 32))
        so[p] = jnp.where(even, lanes(two, -32), one)


def third_kernel(swap, re, ro, upd, out, buf, flat, sems):
    grid = Grid()
    group = grid.lane // 32
    even = group % 2 == 0
    row = grid.sub * 4 + group
    moves = jnp.zeros((8, 128), jnp.int32)
    for b in range(32):
        moves = jnp.where(row == b, swap[b], moves)
    moves = moves > 0
    for v in range(3):
        for i in range(25 * v, 25 * v + 25):
            e, o = re[i // 2], ro[i // 2]
            if i % 2:
                e, o = lanes(e, -32), lanes(o, 32)
            buf[i] = jnp.where(moves, jnp.where(even, e, o), upd[i])
        flat[v] = buf[25 * v : 25 * v + 25].reshape(25, 1024)
        pltpu.make_async_copy(flat.at[v], out.at[v], sems.at[v]).start()
    for v in range(3):
        pltpu.make_async_copy(flat.at[v], out.at[v], sems.at[v]).wait()


VM = pl.BlockSpec(memory_space=pltpu.VMEM)
ANY = pl.BlockSpec(memory_space=pltpu.HBM)
PARAMS = pltpu.CompilerParams(vmem_limit_bytes=40 * 1024 * 1024)


def in_hbm(x):
    return pltpu.with_memory_space_constraint(x, pltpu.HBM)


def planes(*counts):
    return [jax.ShapeDtypeStruct((c, 8, 128), F32) for c in counts]


def local(sea_state, water_depth, neighbours, neighbour_owner, clusters, block_swap):
    devices = lax.axis_size("curve")
    odd_swap = [(i, i + 1) for i in range(1, devices - 1, 2)] + [(i + 1, i) for i in range(1, devices - 1, 2)]
    chip_swap = [(i, i ^ 1) for i in range(devices)]
    far = devices // 2

    def passed(x, pairs):
        return lax.ppermute(x, "curve", pairs)

    ex, eo, ps, u, tr1, tr2, nf, cc, facts = pl.pallas_call(
        first_kernel,
        out_shape=planes(7, 7)
        + [jax.ShapeDtypeStruct((8 * PLANES, 128), F32), jax.ShapeDtypeStruct((5, 75, 8, 128), F32)]
        + planes(48, 48, 60, 20)
        + [jax.ShapeDtypeStruct((8, 8, 128), jnp.int32)],
        in_specs=[ANY] * 5,
        out_specs=[VM] * 9,
        scratch_shapes=[
            pltpu.VMEM((3, 25, 1024), F32),
            pltpu.VMEM((25, 1024), F32),
            pltpu.VMEM((4, 1024), jnp.int32),
            pltpu.VMEM((4, 1024), jnp.int32),
            pltpu.VMEM((8, 128), jnp.int32),
            pltpu.VMEM((4, 8, 128), jnp.int32),
            pltpu.VMEM((4, 8, 128), jnp.int32),
            pltpu.SemaphoreType.DMA((5,)),
        ],
        compiler_params=PARAMS,
        name="predict",
    )(*(in_hbm(x) for x in (sea_state, water_depth, neighbours, neighbour_owner, clusters.reshape(8, 128))))
    es, cb = pl.pallas_call(
        messages_kernel,
        out_shape=planes(9, 75),
        in_specs=[VM] * 3,
        out_specs=[VM] * 2,
        compiler_params=PARAMS,
        cost_estimate=pl.CostEstimate(flops=2_000_000, bytes_accessed=4_000_000, transcendentals=0),
        name="messages",
    )(ps, u, facts)
    ro = passed(eo, odd_swap)
    rx = passed(ex, chip_swap)
    es = lax.dynamic_update_slice(lax.dynamic_update_slice(es, ro[5:], (7, 0, 0)), rx[5:], (5, 0, 0))
    rs = passed(es, [(i, (i + far) % devices) for i in range(devices)])
    hx = pl.pallas_call(
        sides_kernel,
        out_shape=jax.ShapeDtypeStruct((8 * IN_ALL, 128), F32),
        in_specs=[VM] * 3,
        out_specs=VM,
        compiler_params=PARAMS,
        cost_estimate=pl.CostEstimate(flops=2_000_000, bytes_accessed=4_000_000, transcendentals=0),
        name="sides",
    )(rx, ro, facts)
    upd, se, so, _ = pl.pallas_call(
        second_kernel,
        out_shape=planes(75, 38, 38) + [jax.ShapeDtypeStruct((8 * IN_ALL, 128), F32)],
        in_specs=[VM] * 11,
        out_specs=[VM] * 4,
        input_output_aliases={10: 3},
        scratch_shapes=[
            pltpu.VMEM((8 * 160, 128), F32),
            pltpu.VMEM((5, 75, 8, 128), F32),
            pltpu.VMEM((4, 75, 8, 128), F32),
            pltpu.VMEM((4, 75, 8, 128), F32),
            pltpu.VMEM((48, 8, 128), F32),
            pltpu.VMEM((60, 8, 128), F32),
            pltpu.VMEM((30, 8, 128), F32),
            pltpu.VMEM((20, 8, 128), F32),
        ],
        compiler_params=PARAMS,
        name="correct",
    )(rx, ro, rs, ps, cb, tr1, tr2, nf, cc, facts, hx)
    got_odd = passed(so, odd_swap)
    got_even = passed(se, chip_swap)
    return pl.pallas_call(
        third_kernel,
        out_shape=jax.ShapeDtypeStruct((3, 25, 1024), F32),
        in_specs=[pl.BlockSpec(memory_space=pltpu.SMEM)] + [VM] * 3,
        out_specs=ANY,
        scratch_shapes=[
            pltpu.VMEM((75, 8, 128), F32),
            pltpu.VMEM((3, 25, 1024), F32),
            pltpu.SemaphoreType.DMA((3,)),
        ],
        compiler_params=PARAMS,
        name="migrate",
    )(block_swap, got_even, got_odd, upd)


def solution(mesh):
    return jax.shard_map(
        local,
        mesh=mesh,
        in_specs=(
            P(None, None, "curve"),
            P(None, "curve"),
            P(None, "curve"),
            P(None, "curve"),
            P("curve"),
            P("curve"),
        ),
        out_specs=P(None, None, "curve"),
        check_vma=False,
    )
```

```python
import jax
import jax.numpy as jnp
import numpy as np
from jax import lax
from jax.experimental import pallas as pl
from jax.experimental.pallas import tpu as pltpu
from jax.sharding import PartitionSpec as P

F32 = jnp.float32
FACES = ((0, 5, 10, 15, 20), (4, 9, 14, 19, 24), (0, 1, 2, 3, 4), (20, 21, 22, 23, 24))
EDGE = tuple(sorted({n for face in FACES for n in face}))
PLACE = {n: i for i, n in enumerate(EDGE)}
LIFT = 0.06 * 10.0 * 0.5
RATIO = (1.0 / 8.0, 1.0 / 6.0, 1.0 / 8.0)
HALF, SECOND, WHOLE = (0.5, 1.0, 1.0, 1.0), (0.5, 3.0, 7.0, 15.0), (1.0, 4.0, 8.0, 16.0)
AT_DEPTH, AT_FLAG, AT_X, AT_X2, AT_Y, AT_Y2, PLANES = 75, 100, 104, 120, 136, 152, 168
IN_FACE, IN_SECOND, IN_SIDE, IN_ALL = 104, 120, 136, 152
VALUES = [i for i in range(IN_ALL) if i < 101 or (i >= 104 and (i - 104) % 16 < 15)]


def derivative_matrix():
    points = np.array([-1.0, -np.sqrt(3.0 / 7.0), 0.0, np.sqrt(3.0 / 7.0), 1.0])
    gaps = points[:, None] - points[None, :] + np.eye(5)
    weights = 1.0 / gaps.prod(axis=1)
    matrix = weights[None, :] / weights[:, None] / gaps
    matrix -= np.diag(np.diag(matrix))
    return matrix - np.diag(matrix.sum(axis=1))


STEP = -0.06 * derivative_matrix()


def slope(f, scale, ends=False):
    step = scale * STEP
    even_a, even_b, odd_a, odd_b = f[0] + f[4], f[1] + f[3], f[0] - f[4], f[1] - f[3]
    twice = f[2] + f[2]
    even_a, even_b = even_a - twice, even_b - twice
    out = [None] * 5
    for i in (0,) if ends else (0, 1):
        minus = float(step[i, 0] + step[i, 4]) * 0.5 * even_a + float(step[i, 1] + step[i, 3]) * 0.5 * even_b
        plus = float(step[i, 0] - step[i, 4]) * 0.5 * odd_a + float(step[i, 1] - step[i, 3]) * 0.5 * odd_b
        out[i], out[4 - i] = plus + minus, plus - minus
    if not ends:
        out[2] = float(step[2, 0]) * odd_a + float(step[2, 1]) * odd_b
    return out


def operate(src, dst, depth, scale=1.0, axis=None):
    for j in range(5):
        if axis == 1 and 0 < j < 4:
            continue
        line = [5 * j + i for i in range(5)]
        grad = slope([src[n] for n in line], scale, axis == 0)
        part = slope([src[25 + n] for n in line], scale, axis == 0)
        for i, n in enumerate(line):
            if grad[i] is not None:
                dst[25 + n] = depth(n) * grad[i]
                dst[n] = part[i]
    for i in range(5):
        if axis == 0 and 0 < i < 4:
            continue
        line = [5 * j + i for j in range(5)]
        grad = slope([src[n] for n in line], scale, axis == 1)
        part = slope([src[50 + n] for n in line], scale, axis == 1)
        for j, n in enumerate(line):
            if grad[j] is not None:
                dst[50 + n] = depth(n) * grad[j]
                dst[n] = dst[n] + part[j]


def weighted(values, weights):
    total = None
    for value, weight in zip(values, weights):
        value = value if weight == 1.0 else weight * value
        total = value if total is None else total + value
    return total


def lanes(x, by):
    return x if by % 128 == 0 else pltpu.roll(x, by % 128, 1)


def subs(x, by):
    return pltpu.roll(x, by % 8, 0)


class Grid:
    def __init__(self):
        self.lane = lax.broadcasted_iota(jnp.int32, (8, 128), 1)
        self.sub = lax.broadcasted_iota(jnp.int32, (8, 128), 0)
        self.col = self.lane % 32
        self.west = self.col < 16
        self.south = self.sub < 4

    def across(self, x, face):
        if face == 0:
            return lanes(x, 1)
        if face == 1:
            return lanes(x, -1)
        if face == 2:
            y = lanes(x, 32)
            return jnp.where(self.lane < 32, subs(y, 1), y)
        y = lanes(x, -32)
        return jnp.where(self.lane >= 96, subs(y, -1), y)


def spread_ints(ref, out):
    for j in range(8):
        out[:, j, :] = ref[:, 128 * j : 128 * j + 128]


def face_facts(near, owner, facts):
    me = lax.axis_index("curve")
    odd = me % 2
    chip = me + 1 - 2 * odd
    swap = me - 1 + 2 * odd
    for f in range(4):
        wall = near[f] < 0
        remote = (near[f] >= 0) & (owner[f] != me)
        peer = jnp.where(remote, owner[f], -1).astype(F32)
        peer = jnp.max(jnp.max(peer, axis=1, keepdims=True), axis=0, keepdims=True).astype(jnp.int32)
        peer = jnp.broadcast_to(peer, (8, 128))
        slot = jnp.where(peer == chip, 0, jnp.where(peer == swap, 1, 2))
        facts[f] = jnp.where(peer < 0, 3, slot)
        facts[4 + f] = jnp.where(wall, 1, jnp.where(remote, 2, 0))


def read_facts(facts):
    walls = [facts[4 + f] == 1 for f in range(4)]
    remotes = [facts[4 + f] == 2 for f in range(4)]
    return walls, remotes, [facts[f] for f in range(4)]


def flux(js, jn, jt, speed, depth, sign):
    lifted = LIFT * speed
    turn = LIFT * sign
    return lifted * js - turn * jn, lifted * jn - depth * (turn * js), lifted * jt


def side_edges(grid, get):
    blank = jnp.zeros((8, 128), F32)
    west, east = [blank] * 5, [blank] * 5
    for i in VALUES:
        a, by = divmod(i, 32)
        by = 2 * by if by < 16 else 2 * by - 31
        turned = lanes(get(i), by)
        west[a] = jnp.where(grid.col == by, turned, west[a])
        east[a] = jnp.where(grid.col == (31 + by) % 32, turned, east[a])
    return west, [lanes(x, -31) for x in east]


def row_edges(grid, ps):
    blank = jnp.zeros((8, 128), F32)
    south, north = [blank] * 5, [blank] * 5
    for group in range(IN_ALL // 8):
        a, g = divmod(group, 4)
        base = {13: 17, 14: 18, 15: 19, 16: 20, 17: 13, 18: 14}.get(group, group)
        here = grid.lane // 32 == g
        low = ps[pl.ds(64 * base, 8, stride=8), :]
        high = ps[pl.ds(64 * base + 7, 8, stride=8), :]
        south[a] = jnp.where(here, lanes(low, 32 * g), south[a])
        north[a] = jnp.where(here, lanes(high, 32 * g + 32), north[a])
    return south, north


def first_kernel(
    sea_in, dep_in, near_in, owner_in, cl_in, ex, eo, ps, u, tr1, tr2, nf, cc, facts, sea, dep, nb, ow, cl, near, owner, change, sems
):
    copies = [
        pltpu.make_async_copy(src, dst, sems.at[i])
        for i, (src, dst) in enumerate(((sea_in, sea), (dep_in, dep), (near_in, nb), (owner_in, ow), (cl_in, cl)))
    ]
    for copy in copies:
        copy.start()
    grid = Grid()
    lane, sub, col = grid.lane, grid.sub, grid.col
    for copy in copies:
        copy.wait()
    spread_ints(nb, near)
    spread_ints(ow, owner)
    face_facts(near, owner, facts)
    walls, remotes, slots = read_facts(facts)
    inner = [~(walls[f] | remotes[f]) for f in range(4)]
    u[0] = sea[...].reshape(75, 8, 128)
    ps[8 * AT_DEPTH : 8 * AT_FLAG, :] = dep[...].reshape(25, 8, 128).reshape(200, 128)

    def put(p, value):
        ps[8 * p : 8 * p + 8, :] = value

    def get(p):
        return ps[8 * p : 8 * p + 8, :]

    def depth(n):
        return get(AT_DEPTH + n)

    for k in range(3):
        operate(u.at[k], u.at[k + 1], depth, RATIO[k])
    for v in range(3):
        for n in range(25):
            terms = [u[k, 25 * v + n] for k in range(4)]
            u[4, 25 * v + n] = weighted(terms, HALF)
            if n in PLACE:
                tr1[16 * v + PLACE[n]] = weighted(terms, HALF)
                tr2[16 * v + PLACE[n]] = weighted(terms, SECOND)
    operate(u.at[4], change, depth)
    for i in range(75):
        put(i, u[0, i] + change[i])
    for f in range(4):
        sign = -1.0 if f % 2 == 0 else 1.0
        normal, tangent = (1, 2) if f < 2 else (2, 1)
        echo = jnp.where(walls[f], -2.0, 0.0)
        for k in range(5):
            n, opposite = FACES[f][k], FACES[f ^ 1][k]
            a = [tr1[16 * v + PLACE[n]] for v in range(3)]
            b = [grid.across(tr1[16 * v + PLACE[opposite]], f) for v in range(3)]
            for v in range(3):
                nf[15 * f + 5 * v + k] = b[v]
            own = depth(n)
            other = jnp.where(inner[f], grid.across(depth(opposite), f), own)
            speed = jnp.sqrt(jnp.maximum(own, other))
            cc[5 * f + k] = speed
            js = jnp.where(inner[f], b[0] - a[0], 0.0)
            jn = jnp.where(inner[f], b[normal] - a[normal], echo * a[normal])
            jt = jnp.where(inner[f], b[tangent] - a[tangent], 0.0)
            out = flux(js, jn, jt, speed, own, sign)
            for v, part in ((0, out[0]), (normal, out[1]), (tangent, out[2])):
                put(25 * v + n, get(25 * v + n) + part)
    put(AT_FLAG, jnp.where(cl[...] == 0, 1.0, 0.0))
    for v in range(3):
        for k in range(5):
            i = 5 * v + k
            for src, x, y in ((tr1, AT_X, AT_Y), (tr2, AT_X2, AT_Y2)):
                at = [src[16 * v + PLACE[FACES[f][k]]] for f in range(4)]
                put(x + i, jnp.where(grid.west, at[0], at[1]))
                put(y + i, jnp.where(grid.south, at[2], at[3]))
    west, east = side_edges(grid, get)
    for slot, out in ((0, ex), (1, eo)):
        for a in range(5):
            out[a] = jnp.where(slots[0] == slot, west[a], east[a])
    turned = jnp.max(jnp.where((slots[2] < 2) | (slots[3] < 2), 1.0, 0.0)) > 0.5

    @pl.when(turned)
    def _():
        south, north = row_edges(grid, ps)
        for slot, out in ((0, ex), (1, eo)):
            for a in range(5):
                out[a] = jnp.where(slots[2] == slot, south[a], jnp.where(slots[3] == slot, north[a], out[a]))

    blank = jnp.zeros((8, 128), F32)
    corner = ((col == 0) | (col == 31)) & (((sub == 0) & (lane < 32)) | ((sub == 7) & (lane >= 96)))
    for which, at, low, high, mask in ((0, AT_Y, 2, 3, grid.south), (1, AT_X, 0, 1, grid.west)):
        total = blank
        for i in range(20):
            value = get(at + i) if i < 15 else jnp.where(mask, depth(FACES[low][i - 15]), depth(FACES[high][i - 15]))
            total = total + lanes(jnp.where(corner, value, 0.0), i)
        ex[5 + which] = total
        eo[5 + which] = total


def messages_kernel(ps, u, facts, es, cb, whole):
    grid = Grid()
    _, _, slots = read_facts(facts)
    south, north = row_edges(grid, ps)
    for a in range(5):
        es[a] = jnp.where(slots[2] == 2, south[a], north[a])
    for i in range(75):
        whole[i] = weighted([u[k, i] for k in range(4)], WHOLE)
    operate(whole, cb, lambda n: ps[8 * (AT_DEPTH + n) : 8 * (AT_DEPTH + n) + 8, :])
    for i in range(75):
        cb[i] = cb[i] + u[0, i]
    turned = jnp.max(jnp.where((slots[0] == 2) | (slots[1] == 2), 1.0, 0.0)) > 0.5

    @pl.when(turned)
    def _():
        west, east = side_edges(grid, lambda p: ps[8 * p : 8 * p + 8, :])
        for a in range(5):
            es[a] = jnp.where(slots[0] == 2, west[a], jnp.where(slots[1] == 2, east[a], es[a]))


def unpack_sides(grid, got, hx):
    for a in range(5):
        pair = (
            jnp.where(grid.lane % 2 == 0, got[0][a], lanes(got[1][a], 31)),
            jnp.where(grid.lane % 2 == 0, lanes(got[0][a], -1), lanes(got[1][a], 30)),
        )
        for i in VALUES:
            if i // 32 == a:
                hx[8 * i : 8 * i + 8, :] = lanes(pair[i % 32 // 16], -2 * (i % 16))


def sides_kernel(rx, ro, facts, hx):
    _, _, slots = read_facts(facts)
    unpack_sides(Grid(), [[jnp.where(slots[f] == 0, rx[a], ro[a]) for a in range(5)] for f in (0, 1)], hx)


def second_kernel(
    rx, ro, rs, ps, cb, tr1, tr2, nf, cc, facts, hx_in, upd, se, so, hx, hy, m, gx, gy, late, before, after, fast
):
    grid = Grid()
    lane, sub = grid.lane, grid.sub
    walls, remotes, slots = read_facts(facts)

    def get(p):
        return ps[8 * p : 8 * p + 8, :]

    def depth(n):
        return get(AT_DEPTH + n)

    got = [
        [jnp.where(slots[f] == 0, rx[a], jnp.where(slots[f] == 1, ro[a], rs[a])) for a in range(5)] for f in range(4)
    ]
    turned = jnp.max(jnp.where((slots[0] == 2) | (slots[1] == 2), 1.0, 0.0)) > 0.5

    @pl.when(turned)
    def _():
        unpack_sides(grid, got, hx)

    for group in range(IN_ALL // 8):
        a, q = divmod(group, 4)
        hy[pl.ds(64 * group, 8, stride=8), :] = lanes(got[2][a], -32 * q)
        hy[pl.ds(64 * group + 7, 8, stride=8), :] = lanes(got[3][a], 96 - 32 * q)

    def diagonal(f, h, which):
        slot = jnp.where(slots[f] == 2, slots[h], slots[f])
        return jnp.where(slot == 0, rs[5 + which], rs[7 + which])

    there = [[(slots[f] < 3) & (slots[h] < 3) for h in (2, 3)] for f in (0, 1)]
    low, high = sub == 0, sub == 7
    corners = []
    for which in (0, 1):
        corners.append(
            jnp.where(
                grid.south,
                subs(jnp.where(lane < 25, lanes(diagonal(0, 2, which), 1), lanes(diagonal(1, 2, which), 63)), 1),
                subs(
                    jnp.where(
                        (lane >= 96) & (lane < 120), lanes(diagonal(0, 3, which), 65), lanes(diagonal(1, 3, which), 127)
                    ),
                    -1,
                ),
            )
        )
    corner_w = (low & (lane == 0) & there[0][0]) | (high & (lane == 96) & there[0][1])
    corner_e = (low & (lane == 31) & there[1][0]) | (high & (lane == 127) & there[1][1])
    corner_s = low & (corner_w | corner_e)
    corner_n = high & (corner_w | corner_e)

    for i in range(75):
        m[0, i] = get(i)
    for axis, h, g, side, at in ((0, hx, gx, grid.west, AT_X), (1, hy, gy, grid.south, AT_Y)):
        first, last = 2 * axis, 2 * axis + 1
        normal, tangent = (2, 1) if axis else (1, 2)
        sign = jnp.where(side, 1.0, -1.0)

        def halo(p, h=h):
            return h[8 * p : 8 * p + 8, :]

        def halo_depth(n, halo=halo):
            return halo(AT_DEPTH + n)

        for i in range(75):
            g[0, i] = halo(i)
        for k in range(5):
            n, opposite = FACES[first][k], FACES[last][k]
            a = [halo(IN_FACE + 5 * v + k) for v in range(3)]
            b = [get(at + 5 * v + k) for v in range(3)]
            own = jnp.where(side, depth(n), depth(opposite))
            other = jnp.where(side, halo_depth(opposite), halo_depth(n))
            speed = jnp.sqrt(jnp.maximum(own, other))
            j = [b[v] - a[v] for v in range(3)]
            out = flux(j[0], j[normal], j[tangent], speed, other, sign)
            for v, part in ((0, out[0]), (normal, out[1]), (tangent, out[2])):
                g[0, 25 * v + opposite] = g[0, 25 * v + opposite] + jnp.where(side, part, 0.0)
                g[0, 25 * v + n] = g[0, 25 * v + n] + jnp.where(side, 0.0, part)
            out = flux(-j[0], -j[normal], -j[tangent], speed, own, -sign)
            for f in (first, last):
                node = FACES[f][k]
                fast[5 * f + k] = jnp.where(remotes[f], speed, cc[5 * f + k])
                for v in range(3):
                    before[15 * f + 5 * v + k] = jnp.where(remotes[f], a[v], nf[15 * f + 5 * v + k])
                for v, part in ((0, out[0]), (normal, out[1]), (tangent, out[2])):
                    m[0, 25 * v + node] = m[0, 25 * v + node] + jnp.where(remotes[f], part, 0.0)
        first, last = 2 - first, 3 - first
        on_first, on_last = (corner_w, corner_e) if axis else (corner_s, corner_n)
        side = grid.west if axis else grid.south
        sign = jnp.where(side, -1.0, 1.0)
        for k in range(5):
            a = [halo(IN_SIDE + 5 * v + k) for v in range(3)]
            b = [lanes(corners[axis], -(5 * v + k)) for v in range(3)]
            own = jnp.where(side, halo_depth(FACES[first][k]), halo_depth(FACES[last][k]))
            speed = jnp.sqrt(jnp.maximum(own, lanes(corners[axis], -(15 + k))))
            j = [b[v] - a[v] for v in range(3)]
            out = flux(j[0], j[tangent], j[normal], speed, own, sign)
            for v, part in ((0, out[0]), (tangent, out[1]), (normal, out[2])):
                for f, mask in ((first, on_first), (last, on_last)):
                    at_node = 25 * v + FACES[f][k]
                    g[0, at_node] = g[0, at_node] + jnp.where(mask, part, 0.0)
        for k in range(3):
            operate(g.at[k], g.at[k + 1], halo_depth, RATIO[k], axis if k == 2 else None)
        side = grid.south if axis else grid.west
        halo_fine = halo(AT_FLAG) > 0.5
        for v in range(3):
            for k in range(5):
                n, opposite = FACES[2 * axis][k], FACES[2 * axis + 1][k]
                terms = [jnp.where(side, g[q, 25 * v + opposite], g[q, 25 * v + n]) for q in range(4)]
                after[15 * axis + 5 * v + k] = jnp.where(
                    halo_fine, weighted(terms, HALF), halo(IN_SECOND + 5 * v + k)
                )

    for k in range(3):
        operate(m.at[k], m.at[k + 1], depth, RATIO[k])
    for v in range(3):
        for n in range(25):
            value = weighted([m[k, 25 * v + n] for k in range(4)], HALF)
            m[4, 25 * v + n] = value
            if n in PLACE:
                late[16 * v + PLACE[n]] = value
    operate(m.at[4], m.at[1], depth)
    fine = get(AT_FLAG) > 0.5
    for i in range(75):
        upd[i] = jnp.where(fine, m[0, i] + m[1, i], cb[i])
    for f in range(4):
        sign = -1.0 if f % 2 == 0 else 1.0
        axis = f // 2
        normal, tangent = (2, 1) if axis else (1, 2)
        for k in range(5):
            n, opposite = FACES[f][k], FACES[f ^ 1][k]
            speed = fast[5 * f + k]
            j, a_list = [], []
            for v in range(3):
                at, across = 16 * v + PLACE[n], 16 * v + PLACE[opposite]
                a = jnp.where(fine, late[at], tr1[at] + tr2[at])
                sent = grid.across(jnp.where(fine, late[across], tr2[across]), f)
                sent = jnp.where(remotes[f], after[15 * axis + 5 * v + k], sent)
                b = jnp.where(fine, sent, before[15 * f + 5 * v + k] + sent)
                a_list.append(a)
                j.append(b - a)
            js = jnp.where(walls[f], 0.0, j[0])
            jn = jnp.where(walls[f], -2.0 * a_list[normal], j[normal])
            jt = jnp.where(walls[f], 0.0, j[tangent])
            out = flux(js, jn, jt, speed, depth(n), sign)
            for v, part in ((0, out[0]), (normal, out[1]), (tangent, out[2])):
                upd[25 * v + n] = upd[25 * v + n] + part
    even = (lane // 32) % 2 == 0
    for p in range(38):
        one = upd[2 * p]
        two = upd[min(2 * p + 1, 74)]
        se[p] = jnp.where(even, one, lanes(two, 32))
        so[p] = jnp.where(even, lanes(two, -32), one)


def third_kernel(swap, re, ro, upd, out, buf, flat, sems):
    grid = Grid()
    group = grid.lane // 32
    even = group % 2 == 0
    row = grid.sub * 4 + group
    moves = jnp.zeros((8, 128), jnp.int32)
    for b in range(32):
        moves = jnp.where(row == b, swap[b], moves)
    moves = moves > 0
    for v in range(3):
        for i in range(25 * v, 25 * v + 25):
            e, o = re[i // 2], ro[i // 2]
            if i % 2:
                e, o = lanes(e, -32), lanes(o, 32)
            buf[i] = jnp.where(moves, jnp.where(even, e, o), upd[i])
        flat[v] = buf[25 * v : 25 * v + 25].reshape(25, 1024)
        pltpu.make_async_copy(flat.at[v], out.at[v], sems.at[v]).start()
    for v in range(3):
        pltpu.make_async_copy(flat.at[v], out.at[v], sems.at[v]).wait()


VM = pl.BlockSpec(memory_space=pltpu.VMEM)
ANY = pl.BlockSpec(memory_space=pltpu.HBM)
PARAMS = pltpu.CompilerParams(vmem_limit_bytes=40 * 1024 * 1024)


def in_hbm(x):
    return pltpu.with_memory_space_constraint(x, pltpu.HBM)


def planes(*counts):
    return [jax.ShapeDtypeStruct((c, 8, 128), F32) for c in counts]


def local(sea_state, water_depth, neighbours, neighbour_owner, clusters, block_swap):
    devices = lax.axis_size("curve")
    odd_swap = [(i, i + 1) for i in range(1, devices - 1, 2)] + [(i + 1, i) for i in range(1, devices - 1, 2)]
    chip_swap = [(i, i ^ 1) for i in range(devices)]
    far = devices // 2

    def passed(x, pairs):
        return lax.ppermute(x, "curve", pairs)

    ex, eo, ps, u, tr1, tr2, nf, cc, facts = pl.pallas_call(
        first_kernel,
        out_shape=planes(7, 7)
        + [jax.ShapeDtypeStruct((8 * PLANES, 128), F32), jax.ShapeDtypeStruct((5, 75, 8, 128), F32)]
        + planes(48, 48, 60, 20)
        + [jax.ShapeDtypeStruct((8, 8, 128), jnp.int32)],
        in_specs=[ANY] * 5,
        out_specs=[VM] * 9,
        scratch_shapes=[
            pltpu.VMEM((3, 25, 1024), F32),
            pltpu.VMEM((25, 1024), F32),
            pltpu.VMEM((4, 1024), jnp.int32),
            pltpu.VMEM((4, 1024), jnp.int32),
            pltpu.VMEM((8, 128), jnp.int32),
            pltpu.VMEM((4, 8, 128), jnp.int32),
            pltpu.VMEM((4, 8, 128), jnp.int32),
            pltpu.VMEM((75, 8, 128), F32),
            pltpu.SemaphoreType.DMA((5,)),
        ],
        compiler_params=PARAMS,
        name="predict",
    )(*(in_hbm(x) for x in (sea_state, water_depth, neighbours, neighbour_owner, clusters.reshape(8, 128))))
    es, cb = pl.pallas_call(
        messages_kernel,
        out_shape=planes(9, 75),
        in_specs=[VM] * 3,
        out_specs=[VM] * 2,
        scratch_shapes=[pltpu.VMEM((75, 8, 128), F32)],
        compiler_params=PARAMS,
        cost_estimate=pl.CostEstimate(flops=2_000_000, bytes_accessed=4_000_000, transcendentals=0),
        name="messages",
    )(ps, u, facts)
    ro = passed(eo, odd_swap)
    rx = passed(ex, chip_swap)
    es = lax.dynamic_update_slice(lax.dynamic_update_slice(es, ro[5:], (7, 0, 0)), rx[5:], (5, 0, 0))
    rs = passed(es, [(i, (i + far) % devices) for i in range(devices)])
    hx = pl.pallas_call(
        sides_kernel,
        out_shape=jax.ShapeDtypeStruct((8 * IN_ALL, 128), F32),
        in_specs=[VM] * 3,
        out_specs=VM,
        compiler_params=PARAMS,
        cost_estimate=pl.CostEstimate(flops=2_000_000, bytes_accessed=4_000_000, transcendentals=0),
        name="sides",
    )(rx, ro, facts)
    upd, se, so, _ = pl.pallas_call(
        second_kernel,
        out_shape=planes(75, 38, 38) + [jax.ShapeDtypeStruct((8 * IN_ALL, 128), F32)],
        in_specs=[VM] * 11,
        out_specs=[VM] * 4,
        input_output_aliases={10: 3},
        scratch_shapes=[
            pltpu.VMEM((8 * 160, 128), F32),
            pltpu.VMEM((5, 75, 8, 128), F32),
            pltpu.VMEM((4, 75, 8, 128), F32),
            pltpu.VMEM((4, 75, 8, 128), F32),
            pltpu.VMEM((48, 8, 128), F32),
            pltpu.VMEM((60, 8, 128), F32),
            pltpu.VMEM((30, 8, 128), F32),
            pltpu.VMEM((20, 8, 128), F32),
        ],
        compiler_params=PARAMS,
        name="correct",
    )(rx, ro, rs, ps, cb, tr1, tr2, nf, cc, facts, hx)
    got_odd = passed(so, odd_swap)
    got_even = passed(se, chip_swap)
    return pl.pallas_call(
        third_kernel,
        out_shape=jax.ShapeDtypeStruct((3, 25, 1024), F32),
        in_specs=[pl.BlockSpec(memory_space=pltpu.SMEM)] + [VM] * 3,
        out_specs=ANY,
        scratch_shapes=[
            pltpu.VMEM((75, 8, 128), F32),
            pltpu.VMEM((3, 25, 1024), F32),
            pltpu.SemaphoreType.DMA((3,)),
        ],
        compiler_params=PARAMS,
        name="migrate",
    )(block_swap, got_even, got_odd, upd)


def solution(mesh):
    return jax.shard_map(
        local,
        mesh=mesh,
        in_specs=(
            P(None, None, "curve"),
            P(None, "curve"),
            P(None, "curve"),
            P(None, "curve"),
            P("curve"),
            P("curve"),
        ),
        out_specs=P(None, None, "curve"),
        check_vma=False,
    )
```

```python
import jax
import jax.numpy as jnp
import numpy as np
from jax import lax
from jax.experimental import pallas as pl
from jax.experimental.pallas import tpu as pltpu
from jax.sharding import PartitionSpec as P

F32 = jnp.float32
FACES = ((0, 5, 10, 15, 20), (4, 9, 14, 19, 24), (0, 1, 2, 3, 4), (20, 21, 22, 23, 24))
EDGE = tuple(sorted({n for face in FACES for n in face}))
PLACE = {n: i for i, n in enumerate(EDGE)}
LIFT = 0.06 * 10.0 * 0.5
RATIO = (1.0 / 8.0, 1.0 / 6.0, 1.0 / 8.0)
HALF, SECOND, WHOLE = (0.5, 1.0, 1.0, 1.0), (0.5, 3.0, 7.0, 15.0), (1.0, 4.0, 8.0, 16.0)
AT_DEPTH, AT_FLAG, AT_X, AT_X2, AT_Y, AT_Y2, PLANES = 75, 100, 104, 120, 136, 152, 168
IN_FACE, IN_SECOND, IN_SIDE, IN_ALL = 104, 120, 136, 152
VALUES = [i for i in range(IN_ALL) if i < 101 or (i >= 104 and (i - 104) % 16 < 15)]


def derivative_matrix():
    points = np.array([-1.0, -np.sqrt(3.0 / 7.0), 0.0, np.sqrt(3.0 / 7.0), 1.0])
    gaps = points[:, None] - points[None, :] + np.eye(5)
    weights = 1.0 / gaps.prod(axis=1)
    matrix = weights[None, :] / weights[:, None] / gaps
    matrix -= np.diag(np.diag(matrix))
    return matrix - np.diag(matrix.sum(axis=1))


STEP = -0.06 * derivative_matrix()


def slope(f, scale, ends=False):
    step = scale * STEP
    even_a, even_b, odd_a, odd_b = f[0] + f[4], f[1] + f[3], f[0] - f[4], f[1] - f[3]
    twice = f[2] + f[2]
    even_a, even_b = even_a - twice, even_b - twice
    out = [None] * 5
    for i in (0,) if ends else (0, 1):
        minus = float(step[i, 0] + step[i, 4]) * 0.5 * even_a + float(step[i, 1] + step[i, 3]) * 0.5 * even_b
        plus = float(step[i, 0] - step[i, 4]) * 0.5 * odd_a + float(step[i, 1] - step[i, 3]) * 0.5 * odd_b
        out[i], out[4 - i] = plus + minus, plus - minus
    if not ends:
        out[2] = float(step[2, 0]) * odd_a + float(step[2, 1]) * odd_b
    return out


def operate(src, dst, depth, scale=1.0, axis=None):
    for j in range(5):
        if axis == 1 and 0 < j < 4:
            continue
        line = [5 * j + i for i in range(5)]
        grad = slope([src[n] for n in line], scale, axis == 0)
        part = slope([src[25 + n] for n in line], scale, axis == 0)
        for i, n in enumerate(line):
            if grad[i] is not None:
                dst[25 + n] = depth(n) * grad[i]
                dst[n] = part[i]
    for i in range(5):
        if axis == 0 and 0 < i < 4:
            continue
        line = [5 * j + i for j in range(5)]
        grad = slope([src[n] for n in line], scale, axis == 1)
        part = slope([src[50 + n] for n in line], scale, axis == 1)
        for j, n in enumerate(line):
            if grad[j] is not None:
                dst[50 + n] = depth(n) * grad[j]
                dst[n] = dst[n] + part[j]


def weighted(values, weights):
    total = None
    for value, weight in zip(values, weights):
        value = value if weight == 1.0 else weight * value
        total = value if total is None else total + value
    return total


def lanes(x, by):
    return x if by % 128 == 0 else pltpu.roll(x, by % 128, 1)


def subs(x, by):
    return pltpu.roll(x, by % 8, 0)


class Grid:
    def __init__(self):
        self.lane = lax.broadcasted_iota(jnp.int32, (8, 128), 1)
        self.sub = lax.broadcasted_iota(jnp.int32, (8, 128), 0)
        self.col = self.lane % 32
        self.west = self.col < 16
        self.south = self.sub < 4

    def across(self, x, face):
        if face == 0:
            return lanes(x, 1)
        if face == 1:
            return lanes(x, -1)
        if face == 2:
            y = lanes(x, 32)
            return jnp.where(self.lane < 32, subs(y, 1), y)
        y = lanes(x, -32)
        return jnp.where(self.lane >= 96, subs(y, -1), y)


def spread_ints(ref, out):
    for j in range(8):
        out[:, j, :] = ref[:, 128 * j : 128 * j + 128]


def face_facts(near, owner, facts):
    me = lax.axis_index("curve")
    odd = me % 2
    chip = me + 1 - 2 * odd
    swap = me - 1 + 2 * odd
    for f in range(4):
        wall = near[f] < 0
        remote = (near[f] >= 0) & (owner[f] != me)
        peer = jnp.where(remote, owner[f], -1).astype(F32)
        peer = jnp.max(jnp.max(peer, axis=1, keepdims=True), axis=0, keepdims=True).astype(jnp.int32)
        peer = jnp.broadcast_to(peer, (8, 128))
        slot = jnp.where(peer == chip, 0, jnp.where(peer == swap, 1, 2))
        facts[f] = jnp.where(peer < 0, 3, slot)
        facts[4 + f] = jnp.where(wall, 1, jnp.where(remote, 2, 0))


def read_facts(facts):
    walls = [facts[4 + f] == 1 for f in range(4)]
    remotes = [facts[4 + f] == 2 for f in range(4)]
    return walls, remotes, [facts[f] for f in range(4)]


def flux(js, jn, jt, speed, depth, sign):
    lifted = LIFT * speed
    turn = LIFT * sign
    return lifted * js - turn * jn, lifted * jn - depth * (turn * js), lifted * jt


def side_edges(grid, get):
    blank = jnp.zeros((8, 128), F32)
    west, east = [blank] * 5, [blank] * 5
    for i in VALUES:
        a, by = divmod(i, 32)
        by = 2 * by if by < 16 else 2 * by - 31
        turned = lanes(get(i), by)
        west[a] = jnp.where(grid.col == by, turned, west[a])
        east[a] = jnp.where(grid.col == (31 + by) % 32, turned, east[a])
    return west, [lanes(x, -31) for x in east]


def row_edges(grid, ps):
    blank = jnp.zeros((8, 128), F32)
    south, north = [blank] * 5, [blank] * 5
    for group in range(IN_ALL // 8):
        a, g = divmod(group, 4)
        base = {13: 17, 14: 18, 15: 19, 16: 20, 17: 13, 18: 14}.get(group, group)
        here = grid.lane // 32 == g
        low = ps[pl.ds(64 * base, 8, stride=8), :]
        high = ps[pl.ds(64 * base + 7, 8, stride=8), :]
        south[a] = jnp.where(here, lanes(low, 32 * g), south[a])
        north[a] = jnp.where(here, lanes(high, 32 * g + 32), north[a])
    return south, north


def first_kernel(
    sea_in, dep_in, near_in, owner_in, cl_in, ex, eo, ps, u, tr1, tr2, nf, cc, facts, sea, dep, nb, ow, cl, near, owner, change, sems
):
    copies = [
        pltpu.make_async_copy(src, dst, sems.at[i])
        for i, (src, dst) in enumerate(((sea_in, sea), (dep_in, dep), (near_in, nb), (owner_in, ow), (cl_in, cl)))
    ]
    for copy in copies:
        copy.start()
    grid = Grid()
    lane, sub, col = grid.lane, grid.sub, grid.col
    for copy in copies:
        copy.wait()
    spread_ints(nb, near)
    spread_ints(ow, owner)
    face_facts(near, owner, facts)
    walls, remotes, slots = read_facts(facts)
    inner = [~(walls[f] | remotes[f]) for f in range(4)]
    u[0] = sea[...].reshape(75, 8, 128)
    ps[8 * AT_DEPTH : 8 * AT_FLAG, :] = dep[...].reshape(25, 8, 128).reshape(200, 128)

    def put(p, value):
        ps[8 * p : 8 * p + 8, :] = value

    def get(p):
        return ps[8 * p : 8 * p + 8, :]

    def depth(n):
        return get(AT_DEPTH + n)

    for k in range(3):
        operate(u.at[k], u.at[k + 1], depth, RATIO[k])
    for v in range(3):
        for n in range(25):
            terms = [u[k, 25 * v + n] for k in range(4)]
            u[4, 25 * v + n] = weighted(terms, HALF)
            if n in PLACE:
                tr1[16 * v + PLACE[n]] = weighted(terms, HALF)
                tr2[16 * v + PLACE[n]] = weighted(terms, SECOND)
    operate(u.at[4], change, depth)
    for i in range(75):
        put(i, u[0, i] + change[i])
    for f in range(4):
        sign = -1.0 if f % 2 == 0 else 1.0
        normal, tangent = (1, 2) if f < 2 else (2, 1)
        echo = jnp.where(walls[f], -2.0, 0.0)
        for k in range(5):
            n, opposite = FACES[f][k], FACES[f ^ 1][k]
            a = [tr1[16 * v + PLACE[n]] for v in range(3)]
            b = [grid.across(tr1[16 * v + PLACE[opposite]], f) for v in range(3)]
            for v in range(3):
                nf[15 * f + 5 * v + k] = b[v]
            own = depth(n)
            other = jnp.where(inner[f], grid.across(depth(opposite), f), own)
            speed = jnp.sqrt(jnp.maximum(own, other))
            cc[5 * f + k] = speed
            js = jnp.where(inner[f], b[0] - a[0], 0.0)
            jn = jnp.where(inner[f], b[normal] - a[normal], echo * a[normal])
            jt = jnp.where(inner[f], b[tangent] - a[tangent], 0.0)
            out = flux(js, jn, jt, speed, own, sign)
            for v, part in ((0, out[0]), (normal, out[1]), (tangent, out[2])):
                put(25 * v + n, get(25 * v + n) + part)
    put(AT_FLAG, jnp.where(cl[...] == 0, 1.0, 0.0))
    for v in range(3):
        for k in range(5):
            i = 5 * v + k
            for src, x, y in ((tr1, AT_X, AT_Y), (tr2, AT_X2, AT_Y2)):
                at = [src[16 * v + PLACE[FACES[f][k]]] for f in range(4)]
                put(x + i, jnp.where(grid.west, at[0], at[1]))
                put(y + i, jnp.where(grid.south, at[2], at[3]))
    blank = jnp.zeros((8, 128), F32)
    corner = ((col == 0) | (col == 31)) & (((sub == 0) & (lane < 32)) | ((sub == 7) & (lane >= 96)))
    for which, at, low, high, mask in ((0, AT_Y, 2, 3, grid.south), (1, AT_X, 0, 1, grid.west)):
        total = blank
        for i in range(20):
            value = get(at + i) if i < 15 else jnp.where(mask, depth(FACES[low][i - 15]), depth(FACES[high][i - 15]))
            total = total + lanes(jnp.where(corner, value, 0.0), i)
        ex[5 + which] = total
        eo[5 + which] = total

    west, east = side_edges(grid, get)
    for slot, out in ((0, ex), (1, eo)):
        for a in range(5):
            out[a] = jnp.where(slots[0] == slot, west[a], east[a])
    turned = jnp.max(jnp.where((slots[2] < 2) | (slots[3] < 2), 1.0, 0.0)) > 0.5

    @pl.when(turned)
    def _():
        south, north = row_edges(grid, ps)
        for slot, out in ((0, ex), (1, eo)):
            for a in range(5):
                out[a] = jnp.where(slots[2] == slot, south[a], jnp.where(slots[3] == slot, north[a], out[a]))


def messages_kernel(ps, u, facts, es, cb, whole):
    grid = Grid()
    _, _, slots = read_facts(facts)
    south, north = row_edges(grid, ps)
    for a in range(5):
        es[a] = jnp.where(slots[2] == 2, south[a], north[a])
    for i in range(75):
        whole[i] = weighted([u[k, i] for k in range(4)], WHOLE)
    operate(whole, cb, lambda n: ps[8 * (AT_DEPTH + n) : 8 * (AT_DEPTH + n) + 8, :])
    for i in range(75):
        cb[i] = cb[i] + u[0, i]
    turned = jnp.max(jnp.where((slots[0] == 2) | (slots[1] == 2), 1.0, 0.0)) > 0.5

    @pl.when(turned)
    def _():
        west, east = side_edges(grid, lambda p: ps[8 * p : 8 * p + 8, :])
        for a in range(5):
            es[a] = jnp.where(slots[0] == 2, west[a], jnp.where(slots[1] == 2, east[a], es[a]))


def unpack_sides(grid, got, hx):
    for a in range(5):
        pair = (
            jnp.where(grid.lane % 2 == 0, got[0][a], lanes(got[1][a], 31)),
            jnp.where(grid.lane % 2 == 0, lanes(got[0][a], -1), lanes(got[1][a], 30)),
        )
        for i in VALUES:
            if i // 32 == a:
                hx[8 * i : 8 * i + 8, :] = lanes(pair[i % 32 // 16], -2 * (i % 16))


def sides_kernel(rx, ro, facts, hx):
    _, _, slots = read_facts(facts)
    unpack_sides(Grid(), [[jnp.where(slots[f] == 0, rx[a], ro[a]) for a in range(5)] for f in (0, 1)], hx)


def second_kernel(
    rx, ro, rs, ps, cb, tr1, tr2, nf, cc, facts, hx_in, upd, se, so, hx, hy, m, gx, gy, late, before, after, fast
):
    grid = Grid()
    lane, sub = grid.lane, grid.sub
    walls, remotes, slots = read_facts(facts)

    def get(p):
        return ps[8 * p : 8 * p + 8, :]

    def depth(n):
        return get(AT_DEPTH + n)

    got = [
        [jnp.where(slots[f] == 0, rx[a], jnp.where(slots[f] == 1, ro[a], rs[a])) for a in range(5)] for f in range(4)
    ]
    turned = jnp.max(jnp.where((slots[0] == 2) | (slots[1] == 2), 1.0, 0.0)) > 0.5
    for group in range(IN_ALL // 8):
        a, q = divmod(group, 4)
        hy[pl.ds(64 * group, 8, stride=8), :] = lanes(got[2][a], -32 * q)
        hy[pl.ds(64 * group + 7, 8, stride=8), :] = lanes(got[3][a], 96 - 32 * q)

    def diagonal(f, h, which):
        slot = jnp.where(slots[f] == 2, slots[h], slots[f])
        return jnp.where(slot == 0, rs[5 + which], rs[7 + which])

    there = [[(slots[f] < 3) & (slots[h] < 3) for h in (2, 3)] for f in (0, 1)]
    low, high = sub == 0, sub == 7
    corners = []
    for which in (0, 1):
        corners.append(
            jnp.where(
                grid.south,
                subs(jnp.where(lane < 25, lanes(diagonal(0, 2, which), 1), lanes(diagonal(1, 2, which), 63)), 1),
                subs(
                    jnp.where(
                        (lane >= 96) & (lane < 120), lanes(diagonal(0, 3, which), 65), lanes(diagonal(1, 3, which), 127)
                    ),
                    -1,
                ),
            )
        )
    corner_w = (low & (lane == 0) & there[0][0]) | (high & (lane == 96) & there[0][1])
    corner_e = (low & (lane == 31) & there[1][0]) | (high & (lane == 127) & there[1][1])
    corner_s = low & (corner_w | corner_e)
    corner_n = high & (corner_w | corner_e)

    for i in range(75):
        m[0, i] = get(i)
    for axis, h, g, side, at in ((1, hy, gy, grid.south, AT_Y), (0, hx, gx, grid.west, AT_X)):
        if axis == 0:

            @pl.when(turned)
            def _():
                unpack_sides(grid, got, hx)

        first, last = 2 * axis, 2 * axis + 1
        normal, tangent = (2, 1) if axis else (1, 2)
        sign = jnp.where(side, 1.0, -1.0)

        def halo(p, h=h):
            return h[8 * p : 8 * p + 8, :]

        def halo_depth(n, halo=halo):
            return halo(AT_DEPTH + n)

        for i in range(75):
            g[0, i] = halo(i)
        for k in range(5):
            n, opposite = FACES[first][k], FACES[last][k]
            a = [halo(IN_FACE + 5 * v + k) for v in range(3)]
            b = [get(at + 5 * v + k) for v in range(3)]
            own = jnp.where(side, depth(n), depth(opposite))
            other = jnp.where(side, halo_depth(opposite), halo_depth(n))
            speed = jnp.sqrt(jnp.maximum(own, other))
            j = [b[v] - a[v] for v in range(3)]
            out = flux(j[0], j[normal], j[tangent], speed, other, sign)
            for v, part in ((0, out[0]), (normal, out[1]), (tangent, out[2])):
                g[0, 25 * v + opposite] = g[0, 25 * v + opposite] + jnp.where(side, part, 0.0)
                g[0, 25 * v + n] = g[0, 25 * v + n] + jnp.where(side, 0.0, part)
            out = flux(-j[0], -j[normal], -j[tangent], speed, own, -sign)
            for f in (first, last):
                node = FACES[f][k]
                fast[5 * f + k] = jnp.where(remotes[f], speed, cc[5 * f + k])
                for v in range(3):
                    before[15 * f + 5 * v + k] = jnp.where(remotes[f], a[v], nf[15 * f + 5 * v + k])
                for v, part in ((0, out[0]), (normal, out[1]), (tangent, out[2])):
                    m[0, 25 * v + node] = m[0, 25 * v + node] + jnp.where(remotes[f], part, 0.0)
        first, last = 2 - first, 3 - first
        on_first, on_last = (corner_w, corner_e) if axis else (corner_s, corner_n)
        side = grid.west if axis else grid.south
        sign = jnp.where(side, -1.0, 1.0)
        for k in range(5):
            a = [halo(IN_SIDE + 5 * v + k) for v in range(3)]
            b = [lanes(corners[axis], -(5 * v + k)) for v in range(3)]
            own = jnp.where(side, halo_depth(FACES[first][k]), halo_depth(FACES[last][k]))
            speed = jnp.sqrt(jnp.maximum(own, lanes(corners[axis], -(15 + k))))
            j = [b[v] - a[v] for v in range(3)]
            out = flux(j[0], j[tangent], j[normal], speed, own, sign)
            for v, part in ((0, out[0]), (tangent, out[1]), (normal, out[2])):
                for f, mask in ((first, on_first), (last, on_last)):
                    at_node = 25 * v + FACES[f][k]
                    g[0, at_node] = g[0, at_node] + jnp.where(mask, part, 0.0)
        for k in range(3):
            operate(g.at[k], g.at[k + 1], halo_depth, RATIO[k], axis if k == 2 else None)
        side = grid.south if axis else grid.west
        halo_fine = halo(AT_FLAG) > 0.5
        for v in range(3):
            for k in range(5):
                n, opposite = FACES[2 * axis][k], FACES[2 * axis + 1][k]
                terms = [jnp.where(side, g[q, 25 * v + opposite], g[q, 25 * v + n]) for q in range(4)]
                after[15 * axis + 5 * v + k] = jnp.where(
                    halo_fine, weighted(terms, HALF), halo(IN_SECOND + 5 * v + k)
                )

    for k in range(3):
        operate(m.at[k], m.at[k + 1], depth, RATIO[k])
    for v in range(3):
        for n in range(25):
            value = weighted([m[k, 25 * v + n] for k in range(4)], HALF)
            m[4, 25 * v + n] = value
            if n in PLACE:
                late[16 * v + PLACE[n]] = value
    operate(m.at[4], m.at[1], depth)
    fine = get(AT_FLAG) > 0.5
    for i in range(75):
        upd[i] = jnp.where(fine, m[0, i] + m[1, i], cb[i])
    for f in range(4):
        sign = -1.0 if f % 2 == 0 else 1.0
        axis = f // 2
        normal, tangent = (2, 1) if axis else (1, 2)
        for k in range(5):
            n, opposite = FACES[f][k], FACES[f ^ 1][k]
            speed = fast[5 * f + k]
            j, a_list = [], []
            for v in range(3):
                at, across = 16 * v + PLACE[n], 16 * v + PLACE[opposite]
                a = jnp.where(fine, late[at], tr1[at] + tr2[at])
                sent = grid.across(jnp.where(fine, late[across], tr2[across]), f)
                sent = jnp.where(remotes[f], after[15 * axis + 5 * v + k], sent)
                b = jnp.where(fine, sent, before[15 * f + 5 * v + k] + sent)
                a_list.append(a)
                j.append(b - a)
            js = jnp.where(walls[f], 0.0, j[0])
            jn = jnp.where(walls[f], -2.0 * a_list[normal], j[normal])
            jt = jnp.where(walls[f], 0.0, j[tangent])
            out = flux(js, jn, jt, speed, depth(n), sign)
            for v, part in ((0, out[0]), (normal, out[1]), (tangent, out[2])):
                upd[25 * v + n] = upd[25 * v + n] + part
    even = (lane // 32) % 2 == 0
    for p in range(38):
        one = upd[2 * p]
        two = upd[min(2 * p + 1, 74)]
        se[p] = jnp.where(even, one, lanes(two, 32))
        so[p] = jnp.where(even, lanes(two, -32), one)


def settle_kernel(swap, re, upd, kept, take):
    grid = Grid()
    group = grid.lane // 32
    even = group % 2 == 0
    row = grid.sub * 4 + group
    moves = jnp.zeros((8, 128), jnp.int32)
    for b in range(32):
        moves = jnp.where(row == b, swap[b], moves)
    moves = moves > 0
    take[0] = jnp.where(moves & ~even, 1.0, 0.0)
    for i in range(75):
        e = lanes(re[i // 2], -32) if i % 2 else re[i // 2]
        kept[i] = jnp.where(moves & even, e, upd[i])


def third_kernel(ro, kept, take, out, buf, flat, sems):
    moves = take[0] > 0.5
    for v in range(3):
        for i in range(25 * v, 25 * v + 25):
            o = lanes(ro[i // 2], 32) if i % 2 else ro[i // 2]
            buf[i] = jnp.where(moves, o, kept[i])
        flat[v] = buf[25 * v : 25 * v + 25].reshape(25, 1024)
        pltpu.make_async_copy(flat.at[v], out.at[v], sems.at[v]).start()
    for v in range(3):
        pltpu.make_async_copy(flat.at[v], out.at[v], sems.at[v]).wait()


VM = pl.BlockSpec(memory_space=pltpu.VMEM)
ANY = pl.BlockSpec(memory_space=pltpu.HBM)
PARAMS = pltpu.CompilerParams(vmem_limit_bytes=40 * 1024 * 1024)


def in_hbm(x):
    return pltpu.with_memory_space_constraint(x, pltpu.HBM)


def planes(*counts):
    return [jax.ShapeDtypeStruct((c, 8, 128), F32) for c in counts]


def local(sea_state, water_depth, neighbours, neighbour_owner, clusters, block_swap):
    devices = lax.axis_size("curve")
    odd_swap = [(i, i + 1) for i in range(1, devices - 1, 2)] + [(i + 1, i) for i in range(1, devices - 1, 2)]
    chip_swap = [(i, i ^ 1) for i in range(devices)]
    far = devices // 2

    def passed(x, pairs):
        return lax.ppermute(x, "curve", pairs)

    ex, eo, ps, u, tr1, tr2, nf, cc, facts = pl.pallas_call(
        first_kernel,
        out_shape=planes(7, 7)
        + [jax.ShapeDtypeStruct((8 * PLANES, 128), F32), jax.ShapeDtypeStruct((5, 75, 8, 128), F32)]
        + planes(48, 48, 60, 20)
        + [jax.ShapeDtypeStruct((8, 8, 128), jnp.int32)],
        in_specs=[ANY] * 5,
        out_specs=[VM] * 9,
        scratch_shapes=[
            pltpu.VMEM((3, 25, 1024), F32),
            pltpu.VMEM((25, 1024), F32),
            pltpu.VMEM((4, 1024), jnp.int32),
            pltpu.VMEM((4, 1024), jnp.int32),
            pltpu.VMEM((8, 128), jnp.int32),
            pltpu.VMEM((4, 8, 128), jnp.int32),
            pltpu.VMEM((4, 8, 128), jnp.int32),
            pltpu.VMEM((75, 8, 128), F32),
            pltpu.SemaphoreType.DMA((5,)),
        ],
        compiler_params=PARAMS,
        name="predict",
    )(*(in_hbm(x) for x in (sea_state, water_depth, neighbours, neighbour_owner, clusters.reshape(8, 128))))
    es, cb = pl.pallas_call(
        messages_kernel,
        out_shape=planes(9, 75),
        in_specs=[VM] * 3,
        out_specs=[VM] * 2,
        scratch_shapes=[pltpu.VMEM((75, 8, 128), F32)],
        compiler_params=PARAMS,
        cost_estimate=pl.CostEstimate(flops=2_000_000, bytes_accessed=4_000_000, transcendentals=0),
        name="messages",
    )(ps, u, facts)
    ro = passed(eo, odd_swap)
    rx = passed(ex, chip_swap)
    es = lax.dynamic_update_slice(lax.dynamic_update_slice(es, ro[5:], (7, 0, 0)), rx[5:], (5, 0, 0))
    rs = passed(es, [(i, (i + far) % devices) for i in range(devices)])
    hx = pl.pallas_call(
        sides_kernel,
        out_shape=jax.ShapeDtypeStruct((8 * IN_ALL, 128), F32),
        in_specs=[VM] * 3,
        out_specs=VM,
        compiler_params=PARAMS,
        cost_estimate=pl.CostEstimate(flops=2_000_000, bytes_accessed=4_000_000, transcendentals=0),
        name="sides",
    )(rx, ro, facts)
    upd, se, so, _ = pl.pallas_call(
        second_kernel,
        out_shape=planes(75, 38, 38) + [jax.ShapeDtypeStruct((8 * IN_ALL, 128), F32)],
        in_specs=[VM] * 11,
        out_specs=[VM] * 4,
        input_output_aliases={10: 3},
        scratch_shapes=[
            pltpu.VMEM((8 * 160, 128), F32),
            pltpu.VMEM((5, 75, 8, 128), F32),
            pltpu.VMEM((4, 75, 8, 128), F32),
            pltpu.VMEM((4, 75, 8, 128), F32),
            pltpu.VMEM((48, 8, 128), F32),
            pltpu.VMEM((60, 8, 128), F32),
            pltpu.VMEM((30, 8, 128), F32),
            pltpu.VMEM((20, 8, 128), F32),
        ],
        compiler_params=PARAMS,
        name="correct",
    )(rx, ro, rs, ps, cb, tr1, tr2, nf, cc, facts, hx)
    got_odd = passed(so, odd_swap)
    got_even = passed(se, chip_swap)
    kept, take = pl.pallas_call(
        settle_kernel,
        out_shape=planes(75, 1),
        in_specs=[pl.BlockSpec(memory_space=pltpu.SMEM)] + [VM] * 2,
        out_specs=[VM] * 2,
        compiler_params=PARAMS,
        cost_estimate=pl.CostEstimate(flops=2_000_000, bytes_accessed=4_000_000, transcendentals=0),
        name="settle",
    )(block_swap, got_even, upd)
    return pl.pallas_call(
        third_kernel,
        out_shape=jax.ShapeDtypeStruct((3, 25, 1024), F32),
        in_specs=[VM] * 3,
        out_specs=ANY,
        scratch_shapes=[
            pltpu.VMEM((75, 8, 128), F32),
            pltpu.VMEM((3, 25, 1024), F32),
            pltpu.SemaphoreType.DMA((3,)),
        ],
        compiler_params=PARAMS,
        name="migrate",
    )(got_odd, kept, take)


def solution(mesh):
    return jax.shard_map(
        local,
        mesh=mesh,
        in_specs=(
            P(None, None, "curve"),
            P(None, "curve"),
            P(None, "curve"),
            P(None, "curve"),
            P("curve"),
            P("curve"),
        ),
        out_specs=P(None, None, "curve"),
        check_vma=False,
    )
```

```python
import jax
import jax.numpy as jnp
import numpy as np
from jax import lax
from jax.experimental import pallas as pl
from jax.experimental.pallas import tpu as pltpu
from jax.sharding import PartitionSpec as P

F32 = jnp.float32
FACES = ((0, 5, 10, 15, 20), (4, 9, 14, 19, 24), (0, 1, 2, 3, 4), (20, 21, 22, 23, 24))
EDGE = tuple(sorted({n for face in FACES for n in face}))
PLACE = {n: i for i, n in enumerate(EDGE)}
LIFT = 0.06 * 10.0 * 0.5
RATIO = (1.0 / 8.0, 1.0 / 6.0, 1.0 / 8.0)
HALF, SECOND, WHOLE = (0.5, 1.0, 1.0, 1.0), (0.5, 3.0, 7.0, 15.0), (1.0, 4.0, 8.0, 16.0)
AT_DEPTH, AT_FLAG, AT_X, AT_X2, AT_Y, AT_Y2, PLANES = 75, 100, 104, 120, 136, 152, 168
IN_FACE, IN_SECOND, IN_SIDE, IN_ALL = 104, 120, 136, 152
VALUES = [i for i in range(IN_ALL) if i < 101 or (i >= 104 and (i - 104) % 16 < 15)]


def derivative_matrix():
    points = np.array([-1.0, -np.sqrt(3.0 / 7.0), 0.0, np.sqrt(3.0 / 7.0), 1.0])
    gaps = points[:, None] - points[None, :] + np.eye(5)
    weights = 1.0 / gaps.prod(axis=1)
    matrix = weights[None, :] / weights[:, None] / gaps
    matrix -= np.diag(np.diag(matrix))
    return matrix - np.diag(matrix.sum(axis=1))


STEP = -0.06 * derivative_matrix()


def slope(f, scale, ends=False):
    step = scale * STEP
    even_a, even_b, odd_a, odd_b = f[0] + f[4], f[1] + f[3], f[0] - f[4], f[1] - f[3]
    twice = f[2] + f[2]
    even_a, even_b = even_a - twice, even_b - twice
    out = [None] * 5
    for i in (0,) if ends else (0, 1):
        minus = float(step[i, 0] + step[i, 4]) * 0.5 * even_a + float(step[i, 1] + step[i, 3]) * 0.5 * even_b
        plus = float(step[i, 0] - step[i, 4]) * 0.5 * odd_a + float(step[i, 1] - step[i, 3]) * 0.5 * odd_b
        out[i], out[4 - i] = plus + minus, plus - minus
    if not ends:
        out[2] = float(step[2, 0]) * odd_a + float(step[2, 1]) * odd_b
    return out


def operate(src, dst, depth, scale=1.0, axis=None):
    for j in range(5):
        if axis == 1 and 0 < j < 4:
            continue
        line = [5 * j + i for i in range(5)]
        grad = slope([src[n] for n in line], scale, axis == 0)
        part = slope([src[25 + n] for n in line], scale, axis == 0)
        for i, n in enumerate(line):
            if grad[i] is not None:
                dst[25 + n] = depth(n) * grad[i]
                dst[n] = part[i]
    for i in range(5):
        if axis == 0 and 0 < i < 4:
            continue
        line = [5 * j + i for j in range(5)]
        grad = slope([src[n] for n in line], scale, axis == 1)
        part = slope([src[50 + n] for n in line], scale, axis == 1)
        for j, n in enumerate(line):
            if grad[j] is not None:
                dst[50 + n] = depth(n) * grad[j]
                dst[n] = dst[n] + part[j]


def weighted(values, weights):
    total = None
    for value, weight in zip(values, weights):
        value = value if weight == 1.0 else weight * value
        total = value if total is None else total + value
    return total


def lanes(x, by):
    return x if by % 128 == 0 else pltpu.roll(x, by % 128, 1)


def subs(x, by):
    return pltpu.roll(x, by % 8, 0)


class Grid:
    def __init__(self):
        self.lane = lax.broadcasted_iota(jnp.int32, (8, 128), 1)
        self.sub = lax.broadcasted_iota(jnp.int32, (8, 128), 0)
        self.col = self.lane % 32
        self.west = self.col < 16
        self.south = self.sub < 4

    def across(self, x, face):
        if face == 0:
            return lanes(x, 1)
        if face == 1:
            return lanes(x, -1)
        if face == 2:
            y = lanes(x, 32)
            return jnp.where(self.lane < 32, subs(y, 1), y)
        y = lanes(x, -32)
        return jnp.where(self.lane >= 96, subs(y, -1), y)


def spread_ints(ref, out):
    for j in range(8):
        out[:, j, :] = ref[:, 128 * j : 128 * j + 128]


def face_facts(near, owner, facts):
    me = lax.axis_index("curve")
    odd = me % 2
    chip = me + 1 - 2 * odd
    swap = me - 1 + 2 * odd
    for f in range(4):
        wall = near[f] < 0
        remote = (near[f] >= 0) & (owner[f] != me)
        peer = jnp.where(remote, owner[f], -1).astype(F32)
        peer = jnp.max(jnp.max(peer, axis=1, keepdims=True), axis=0, keepdims=True).astype(jnp.int32)
        peer = jnp.broadcast_to(peer, (8, 128))
        slot = jnp.where(peer == chip, 0, jnp.where(peer == swap, 1, 2))
        facts[f] = jnp.where(peer < 0, 3, slot)
        facts[4 + f] = jnp.where(wall, 1, jnp.where(remote, 2, 0))


def read_facts(facts):
    walls = [facts[4 + f] == 1 for f in range(4)]
    remotes = [facts[4 + f] == 2 for f in range(4)]
    return walls, remotes, [facts[f] for f in range(4)]


def flux(js, jn, jt, speed, depth, sign):
    lifted = LIFT * speed
    turn = LIFT * sign
    return lifted * js - turn * jn, lifted * jn - depth * (turn * js), lifted * jt


def side_edges(grid, get):
    blank = jnp.zeros((8, 128), F32)
    west, east = [blank] * 5, [blank] * 5
    for i in VALUES:
        a, by = divmod(i, 32)
        by = 2 * by if by < 16 else 2 * by - 31
        turned = lanes(get(i), by)
        west[a] = jnp.where(grid.col == by, turned, west[a])
        east[a] = jnp.where(grid.col == (31 + by) % 32, turned, east[a])
    return west, [lanes(x, -31) for x in east]


def row_edges(grid, ps):
    blank = jnp.zeros((8, 128), F32)
    south, north = [blank] * 5, [blank] * 5
    for group in range(IN_ALL // 8):
        a, g = divmod(group, 4)
        base = {13: 17, 14: 18, 15: 19, 16: 20, 17: 13, 18: 14}.get(group, group)
        here = grid.lane // 32 == g
        low = ps[pl.ds(64 * base, 8, stride=8), :]
        high = ps[pl.ds(64 * base + 7, 8, stride=8), :]
        south[a] = jnp.where(here, lanes(low, 32 * g), south[a])
        north[a] = jnp.where(here, lanes(high, 32 * g + 32), north[a])
    return south, north


def first_kernel(
    sea_in, dep_in, near_in, owner_in, cl_in, ex, eo, ps, u, tr1, tr2, nf, cc, facts, sea, dep, nb, ow, cl, near, owner, change, sems
):
    copies = [
        pltpu.make_async_copy(src, dst, sems.at[i])
        for i, (src, dst) in enumerate(((sea_in, sea), (dep_in, dep), (near_in, nb), (owner_in, ow), (cl_in, cl)))
    ]
    for copy in copies:
        copy.start()
    grid = Grid()
    lane, sub, col = grid.lane, grid.sub, grid.col
    for copy in copies:
        copy.wait()
    spread_ints(nb, near)
    spread_ints(ow, owner)
    face_facts(near, owner, facts)
    walls, remotes, slots = read_facts(facts)
    inner = [~(walls[f] | remotes[f]) for f in range(4)]
    u[0] = sea[...].reshape(75, 8, 128)
    ps[8 * AT_DEPTH : 8 * AT_FLAG, :] = dep[...].reshape(25, 8, 128).reshape(200, 128)

    def put(p, value):
        ps[8 * p : 8 * p + 8, :] = value

    def get(p):
        return ps[8 * p : 8 * p + 8, :]

    def depth(n):
        return get(AT_DEPTH + n)

    for k in range(3):
        operate(u.at[k], u.at[k + 1], depth, RATIO[k])
    for v in range(3):
        for n in range(25):
            terms = [u[k, 25 * v + n] for k in range(4)]
            u[4, 25 * v + n] = weighted(terms, HALF)
            if n in PLACE:
                tr1[16 * v + PLACE[n]] = weighted(terms, HALF)
                tr2[16 * v + PLACE[n]] = weighted(terms, SECOND)
    operate(u.at[4], change, depth)
    for i in range(75):
        put(i, u[0, i] + change[i])
    for f in range(4):
        sign = -1.0 if f % 2 == 0 else 1.0
        normal, tangent = (1, 2) if f < 2 else (2, 1)
        echo = jnp.where(walls[f], -2.0, 0.0)
        for k in range(5):
            n, opposite = FACES[f][k], FACES[f ^ 1][k]
            a = [tr1[16 * v + PLACE[n]] for v in range(3)]
            b = [grid.across(tr1[16 * v + PLACE[opposite]], f) for v in range(3)]
            for v in range(3):
                nf[15 * f + 5 * v + k] = b[v]
            own = depth(n)
            other = jnp.where(inner[f], grid.across(depth(opposite), f), own)
            speed = jnp.sqrt(jnp.maximum(own, other))
            cc[5 * f + k] = speed
            js = jnp.where(inner[f], b[0] - a[0], 0.0)
            jn = jnp.where(inner[f], b[normal] - a[normal], echo * a[normal])
            jt = jnp.where(inner[f], b[tangent] - a[tangent], 0.0)
            out = flux(js, jn, jt, speed, own, sign)
            for v, part in ((0, out[0]), (normal, out[1]), (tangent, out[2])):
                put(25 * v + n, get(25 * v + n) + part)
    put(AT_FLAG, jnp.where(cl[...] == 0, 1.0, 0.0))
    for v in range(3):
        for k in range(5):
            i = 5 * v + k
            for src, x, y in ((tr1, AT_X, AT_Y), (tr2, AT_X2, AT_Y2)):
                at = [src[16 * v + PLACE[FACES[f][k]]] for f in range(4)]
                put(x + i, jnp.where(grid.west, at[0], at[1]))
                put(y + i, jnp.where(grid.south, at[2], at[3]))
    blank = jnp.zeros((8, 128), F32)
    corner = ((col == 0) | (col == 31)) & (((sub == 0) & (lane < 32)) | ((sub == 7) & (lane >= 96)))
    for which, at, low, high, mask in ((0, AT_Y, 2, 3, grid.south), (1, AT_X, 0, 1, grid.west)):
        total = blank
        for i in range(20):
            value = get(at + i) if i < 15 else jnp.where(mask, depth(FACES[low][i - 15]), depth(FACES[high][i - 15]))
            total = total + lanes(jnp.where(corner, value, 0.0), i)
        ex[5 + which] = total
        eo[5 + which] = total

    west, east = side_edges(grid, get)
    for slot, out in ((0, ex), (1, eo)):
        for a in range(5):
            out[a] = jnp.where(slots[0] == slot, west[a], east[a])
    turned = jnp.max(jnp.where((slots[2] < 2) | (slots[3] < 2), 1.0, 0.0)) > 0.5

    @pl.when(turned)
    def _():
        south, north = row_edges(grid, ps)
        for slot, out in ((0, ex), (1, eo)):
            for a in range(5):
                out[a] = jnp.where(slots[2] == slot, south[a], jnp.where(slots[3] == slot, north[a], out[a]))


def messages_kernel(ps, u, facts, es, cb, whole):
    grid = Grid()
    _, _, slots = read_facts(facts)
    south, north = row_edges(grid, ps)
    for a in range(5):
        es[a] = jnp.where(slots[2] == 2, south[a], north[a])
    for i in range(75):
        whole[i] = weighted([u[k, i] for k in range(4)], WHOLE)
    operate(whole, cb, lambda n: ps[8 * (AT_DEPTH + n) : 8 * (AT_DEPTH + n) + 8, :])
    for i in range(75):
        cb[i] = cb[i] + u[0, i]
    turned = jnp.max(jnp.where((slots[0] == 2) | (slots[1] == 2), 1.0, 0.0)) > 0.5

    @pl.when(turned)
    def _():
        west, east = side_edges(grid, lambda p: ps[8 * p : 8 * p + 8, :])
        for a in range(5):
            es[a] = jnp.where(slots[0] == 2, west[a], jnp.where(slots[1] == 2, east[a], es[a]))


def unpack_sides(grid, got, hx):
    for a in range(5):
        pair = (
            jnp.where(grid.lane % 2 == 0, got[0][a], lanes(got[1][a], 31)),
            jnp.where(grid.lane % 2 == 0, lanes(got[0][a], -1), lanes(got[1][a], 30)),
        )
        for i in VALUES:
            if i // 32 == a:
                hx[8 * i : 8 * i + 8, :] = lanes(pair[i % 32 // 16], -2 * (i % 16))


def touch(grid, axis, h, g, m, ps, masks, fast, before):
    first, last = 2 * axis, 2 * axis + 1
    normal, tangent = (2, 1) if axis else (1, 2)
    side, at = (grid.south, AT_Y) if axis else (grid.west, AT_X)
    sign = jnp.where(side, 1.0, -1.0)

    def get(p):
        return ps[8 * p : 8 * p + 8, :]

    def halo(p):
        return h[8 * p : 8 * p + 8, :]

    for i in range(75):
        g[0, i] = halo(i)
    for k in range(5):
        n, opposite = FACES[first][k], FACES[last][k]
        a = [halo(IN_FACE + 5 * v + k) for v in range(3)]
        b = [get(at + 5 * v + k) for v in range(3)]
        own = jnp.where(side, get(AT_DEPTH + n), get(AT_DEPTH + opposite))
        other = jnp.where(side, halo(AT_DEPTH + opposite), halo(AT_DEPTH + n))
        speed = jnp.sqrt(jnp.maximum(own, other))
        j = [b[v] - a[v] for v in range(3)]
        out = flux(j[0], j[normal], j[tangent], speed, other, sign)
        for v, part in ((0, out[0]), (normal, out[1]), (tangent, out[2])):
            g[0, 25 * v + opposite] = g[0, 25 * v + opposite] + jnp.where(side, part, 0.0)
            g[0, 25 * v + n] = g[0, 25 * v + n] + jnp.where(side, 0.0, part)
        out = flux(-j[0], -j[normal], -j[tangent], speed, own, -sign)
        for f in (first, last):
            node = FACES[f][k]
            fast[5 * f + k] = jnp.where(masks[f], speed, fast[5 * f + k])
            for v in range(3):
                before[15 * f + 5 * v + k] = jnp.where(masks[f], a[v], before[15 * f + 5 * v + k])
            for v, part in ((0, out[0]), (normal, out[1]), (tangent, out[2])):
                m[0, 25 * v + node] = m[0, 25 * v + node] + jnp.where(masks[f], part, 0.0)


def sides_kernel(rx, ro, facts, ps, nf, cc, hx, gx, m, before, fast):
    grid = Grid()
    _, remotes, slots = read_facts(facts)
    unpack_sides(grid, [[jnp.where(slots[f] == 0, rx[a], ro[a]) for a in range(5)] for f in (0, 1)], hx)
    for i in range(75):
        m[0, i] = ps[8 * i : 8 * i + 8, :]
    for i in range(60):
        before[i] = nf[i]
    for i in range(20):
        fast[i] = cc[i]
    touch(grid, 0, hx, gx, m, ps, [remotes[f] & (slots[f] != 2) for f in (0, 1)], fast, before)


def second_kernel(
    rx, ro, rs, ps, cb, tr1, tr2, facts, _hx, _gx, _m, _before, _fast, upd, se, so, hx, gx, m, before, fast, hy, gy, late, after
):
    grid = Grid()
    lane, sub = grid.lane, grid.sub
    walls, remotes, slots = read_facts(facts)

    def get(p):
        return ps[8 * p : 8 * p + 8, :]

    def depth(n):
        return get(AT_DEPTH + n)

    got = [
        [jnp.where(slots[f] == 0, rx[a], jnp.where(slots[f] == 1, ro[a], rs[a])) for a in range(5)] for f in range(4)
    ]
    turned = jnp.max(jnp.where((slots[0] == 2) | (slots[1] == 2), 1.0, 0.0)) > 0.5
    for group in range(IN_ALL // 8):
        a, q = divmod(group, 4)
        hy[pl.ds(64 * group, 8, stride=8), :] = lanes(got[2][a], -32 * q)
        hy[pl.ds(64 * group + 7, 8, stride=8), :] = lanes(got[3][a], 96 - 32 * q)

    def diagonal(f, h, which):
        slot = jnp.where(slots[f] == 2, slots[h], slots[f])
        return jnp.where(slot == 0, rs[5 + which], rs[7 + which])

    there = [[(slots[f] < 3) & (slots[h] < 3) for h in (2, 3)] for f in (0, 1)]
    low, high = sub == 0, sub == 7
    corners = []
    for which in (0, 1):
        corners.append(
            jnp.where(
                grid.south,
                subs(jnp.where(lane < 25, lanes(diagonal(0, 2, which), 1), lanes(diagonal(1, 2, which), 63)), 1),
                subs(
                    jnp.where(
                        (lane >= 96) & (lane < 120), lanes(diagonal(0, 3, which), 65), lanes(diagonal(1, 3, which), 127)
                    ),
                    -1,
                ),
            )
        )
    corner_w = (low & (lane == 0) & there[0][0]) | (high & (lane == 96) & there[0][1])
    corner_e = (low & (lane == 31) & there[1][0]) | (high & (lane == 127) & there[1][1])
    corner_s = low & (corner_w | corner_e)
    corner_n = high & (corner_w | corner_e)

    touch(grid, 1, hy, gy, m, ps, remotes, fast, before)

    @pl.when(turned)
    def _():
        unpack_sides(grid, got, hx)
        touch(grid, 0, hx, gx, m, ps, [remotes[f] & (slots[f] == 2) for f in (0, 1)], fast, before)

    for axis, h, g in ((1, hy, gy), (0, hx, gx)):
        first, last = 2 * axis, 2 * axis + 1
        normal, tangent = (2, 1) if axis else (1, 2)

        def halo(p, h=h):
            return h[8 * p : 8 * p + 8, :]

        def halo_depth(n, halo=halo):
            return halo(AT_DEPTH + n)

        first, last = 2 - first, 3 - first
        on_first, on_last = (corner_w, corner_e) if axis else (corner_s, corner_n)
        side = grid.west if axis else grid.south
        sign = jnp.where(side, -1.0, 1.0)
        for k in range(5):
            a = [halo(IN_SIDE + 5 * v + k) for v in range(3)]
            b = [lanes(corners[axis], -(5 * v + k)) for v in range(3)]
            own = jnp.where(side, halo_depth(FACES[first][k]), halo_depth(FACES[last][k]))
            speed = jnp.sqrt(jnp.maximum(own, lanes(corners[axis], -(15 + k))))
            j = [b[v] - a[v] for v in range(3)]
            out = flux(j[0], j[tangent], j[normal], speed, own, sign)
            for v, part in ((0, out[0]), (tangent, out[1]), (normal, out[2])):
                for f, mask in ((first, on_first), (last, on_last)):
                    at_node = 25 * v + FACES[f][k]
                    g[0, at_node] = g[0, at_node] + jnp.where(mask, part, 0.0)
        for k in range(3):
            operate(g.at[k], g.at[k + 1], halo_depth, RATIO[k], axis if k == 2 else None)
        side = grid.south if axis else grid.west
        halo_fine = halo(AT_FLAG) > 0.5
        for v in range(3):
            for k in range(5):
                n, opposite = FACES[2 * axis][k], FACES[2 * axis + 1][k]
                terms = [jnp.where(side, g[q, 25 * v + opposite], g[q, 25 * v + n]) for q in range(4)]
                after[15 * axis + 5 * v + k] = jnp.where(
                    halo_fine, weighted(terms, HALF), halo(IN_SECOND + 5 * v + k)
                )

    for k in range(3):
        operate(m.at[k], m.at[k + 1], depth, RATIO[k])
    for v in range(3):
        for n in range(25):
            value = weighted([m[k, 25 * v + n] for k in range(4)], HALF)
            m[4, 25 * v + n] = value
            if n in PLACE:
                late[16 * v + PLACE[n]] = value
    operate(m.at[4], m.at[1], depth)
    fine = get(AT_FLAG) > 0.5
    for i in range(75):
        upd[i] = jnp.where(fine, m[0, i] + m[1, i], cb[i])
    for f in range(4):
        sign = -1.0 if f % 2 == 0 else 1.0
        axis = f // 2
        normal, tangent = (2, 1) if axis else (1, 2)
        for k in range(5):
            n, opposite = FACES[f][k], FACES[f ^ 1][k]
            speed = fast[5 * f + k]
            j, a_list = [], []
            for v in range(3):
                at, across = 16 * v + PLACE[n], 16 * v + PLACE[opposite]
                a = jnp.where(fine, late[at], tr1[at] + tr2[at])
                sent = grid.across(jnp.where(fine, late[across], tr2[across]), f)
                sent = jnp.where(remotes[f], after[15 * axis + 5 * v + k], sent)
                b = jnp.where(fine, sent, before[15 * f + 5 * v + k] + sent)
                a_list.append(a)
                j.append(b - a)
            js = jnp.where(walls[f], 0.0, j[0])
            jn = jnp.where(walls[f], -2.0 * a_list[normal], j[normal])
            jt = jnp.where(walls[f], 0.0, j[tangent])
            out = flux(js, jn, jt, speed, depth(n), sign)
            for v, part in ((0, out[0]), (normal, out[1]), (tangent, out[2])):
                upd[25 * v + n] = upd[25 * v + n] + part
    even = (lane // 32) % 2 == 0
    for p in range(38):
        one = upd[2 * p]
        two = upd[min(2 * p + 1, 74)]
        se[p] = jnp.where(even, one, lanes(two, 32))
        so[p] = jnp.where(even, lanes(two, -32), one)


def settle_kernel(swap, re, upd, kept, take):
    grid = Grid()
    group = grid.lane // 32
    even = group % 2 == 0
    row = grid.sub * 4 + group
    moves = jnp.zeros((8, 128), jnp.int32)
    for b in range(32):
        moves = jnp.where(row == b, swap[b], moves)
    moves = moves > 0
    take[0] = jnp.where(moves & ~even, 1.0, 0.0)
    for i in range(75):
        e = lanes(re[i // 2], -32) if i % 2 else re[i // 2]
        kept[i] = jnp.where(moves & even, e, upd[i])


def third_kernel(ro, kept, take, out, buf, flat, sems):
    moves = take[0] > 0.5
    for v in range(3):
        for i in range(25 * v, 25 * v + 25):
            o = lanes(ro[i // 2], 32) if i % 2 else ro[i // 2]
            buf[i] = jnp.where(moves, o, kept[i])
        flat[v] = buf[25 * v : 25 * v + 25].reshape(25, 1024)
        pltpu.make_async_copy(flat.at[v], out.at[v], sems.at[v]).start()
    for v in range(3):
        pltpu.make_async_copy(flat.at[v], out.at[v], sems.at[v]).wait()


VM = pl.BlockSpec(memory_space=pltpu.VMEM)
ANY = pl.BlockSpec(memory_space=pltpu.HBM)
PARAMS = pltpu.CompilerParams(vmem_limit_bytes=40 * 1024 * 1024)


def in_hbm(x):
    return pltpu.with_memory_space_constraint(x, pltpu.HBM)


def planes(*counts):
    return [jax.ShapeDtypeStruct((c, 8, 128), F32) for c in counts]


def local(sea_state, water_depth, neighbours, neighbour_owner, clusters, block_swap):
    devices = lax.axis_size("curve")
    odd_swap = [(i, i + 1) for i in range(1, devices - 1, 2)] + [(i + 1, i) for i in range(1, devices - 1, 2)]
    chip_swap = [(i, i ^ 1) for i in range(devices)]
    far = devices // 2

    def passed(x, pairs):
        return lax.ppermute(x, "curve", pairs)

    ex, eo, ps, u, tr1, tr2, nf, cc, facts = pl.pallas_call(
        first_kernel,
        out_shape=planes(7, 7)
        + [jax.ShapeDtypeStruct((8 * PLANES, 128), F32), jax.ShapeDtypeStruct((5, 75, 8, 128), F32)]
        + planes(48, 48, 60, 20)
        + [jax.ShapeDtypeStruct((8, 8, 128), jnp.int32)],
        in_specs=[ANY] * 5,
        out_specs=[VM] * 9,
        scratch_shapes=[
            pltpu.VMEM((3, 25, 1024), F32),
            pltpu.VMEM((25, 1024), F32),
            pltpu.VMEM((4, 1024), jnp.int32),
            pltpu.VMEM((4, 1024), jnp.int32),
            pltpu.VMEM((8, 128), jnp.int32),
            pltpu.VMEM((4, 8, 128), jnp.int32),
            pltpu.VMEM((4, 8, 128), jnp.int32),
            pltpu.VMEM((75, 8, 128), F32),
            pltpu.SemaphoreType.DMA((5,)),
        ],
        compiler_params=PARAMS,
        name="predict",
    )(*(in_hbm(x) for x in (sea_state, water_depth, neighbours, neighbour_owner, clusters.reshape(8, 128))))
    es, cb = pl.pallas_call(
        messages_kernel,
        out_shape=planes(9, 75),
        in_specs=[VM] * 3,
        out_specs=[VM] * 2,
        scratch_shapes=[pltpu.VMEM((75, 8, 128), F32)],
        compiler_params=PARAMS,
        cost_estimate=pl.CostEstimate(flops=2_000_000, bytes_accessed=4_000_000, transcendentals=0),
        name="messages",
    )(ps, u, facts)
    ro = passed(eo, odd_swap)
    rx = passed(ex, chip_swap)
    es = lax.dynamic_update_slice(lax.dynamic_update_slice(es, ro[5:], (7, 0, 0)), rx[5:], (5, 0, 0))
    rs = passed(es, [(i, (i + far) % devices) for i in range(devices)])
    kept_on = [
        jax.ShapeDtypeStruct((8 * IN_ALL, 128), F32),
        jax.ShapeDtypeStruct((4, 75, 8, 128), F32),
        jax.ShapeDtypeStruct((5, 75, 8, 128), F32),
    ] + planes(60, 20)
    sides = pl.pallas_call(
        sides_kernel,
        out_shape=kept_on,
        in_specs=[VM] * 6,
        out_specs=[VM] * 5,
        compiler_params=PARAMS,
        cost_estimate=pl.CostEstimate(flops=2_000_000, bytes_accessed=4_000_000, transcendentals=0),
        name="sides",
    )(rx, ro, facts, ps, nf, cc)
    upd, se, so, *_ = pl.pallas_call(
        second_kernel,
        out_shape=planes(75, 38, 38) + kept_on,
        in_specs=[VM] * 13,
        out_specs=[VM] * 8,
        input_output_aliases={8 + i: 3 + i for i in range(5)},
        scratch_shapes=[
            pltpu.VMEM((8 * 160, 128), F32),
            pltpu.VMEM((4, 75, 8, 128), F32),
            pltpu.VMEM((48, 8, 128), F32),
            pltpu.VMEM((30, 8, 128), F32),
        ],
        compiler_params=PARAMS,
        name="correct",
    )(rx, ro, rs, ps, cb, tr1, tr2, facts, *sides)
    got_odd = passed(so, odd_swap)
    got_even = passed(se, chip_swap)
    kept, take = pl.pallas_call(
        settle_kernel,
        out_shape=planes(75, 1),
        in_specs=[pl.BlockSpec(memory_space=pltpu.SMEM)] + [VM] * 2,
        out_specs=[VM] * 2,
        compiler_params=PARAMS,
        cost_estimate=pl.CostEstimate(flops=2_000_000, bytes_accessed=4_000_000, transcendentals=0),
        name="settle",
    )(block_swap, got_even, upd)
    return pl.pallas_call(
        third_kernel,
        out_shape=jax.ShapeDtypeStruct((3, 25, 1024), F32),
        in_specs=[VM] * 3,
        out_specs=ANY,
        scratch_shapes=[
            pltpu.VMEM((75, 8, 128), F32),
            pltpu.VMEM((3, 25, 1024), F32),
            pltpu.SemaphoreType.DMA((3,)),
        ],
        compiler_params=PARAMS,
        name="migrate",
    )(got_odd, kept, take)


def solution(mesh):
    return jax.shard_map(
        local,
        mesh=mesh,
        in_specs=(
            P(None, None, "curve"),
            P(None, "curve"),
            P(None, "curve"),
            P(None, "curve"),
            P("curve"),
            P("curve"),
        ),
        out_specs=P(None, None, "curve"),
        check_vma=False,
    )
```

```python
import jax
import jax.numpy as jnp
import numpy as np
from jax import lax
from jax.experimental import pallas as pl
from jax.experimental.pallas import tpu as pltpu
from jax.sharding import PartitionSpec as P

F32 = jnp.float32
FACES = ((0, 5, 10, 15, 20), (4, 9, 14, 19, 24), (0, 1, 2, 3, 4), (20, 21, 22, 23, 24))
EDGE = tuple(sorted({n for face in FACES for n in face}))
PLACE = {n: i for i, n in enumerate(EDGE)}
LIFT = 0.06 * 10.0 * 0.5
RATIO = (1.0 / 8.0, 1.0 / 6.0, 1.0 / 8.0)
HALF, SECOND, WHOLE = (0.5, 1.0, 1.0, 1.0), (0.5, 3.0, 7.0, 15.0), (1.0, 4.0, 8.0, 16.0)
AT_DEPTH, AT_FLAG, AT_X, AT_X2, AT_Y, AT_Y2, PLANES = 75, 100, 104, 120, 136, 152, 168
IN_FACE, IN_SECOND, IN_SIDE, IN_ALL = 104, 120, 136, 152
VALUES = [i for i in range(IN_ALL) if i < 101 or (i >= 104 and (i - 104) % 16 < 15)]


def derivative_matrix():
    points = np.array([-1.0, -np.sqrt(3.0 / 7.0), 0.0, np.sqrt(3.0 / 7.0), 1.0])
    gaps = points[:, None] - points[None, :] + np.eye(5)
    weights = 1.0 / gaps.prod(axis=1)
    matrix = weights[None, :] / weights[:, None] / gaps
    matrix -= np.diag(np.diag(matrix))
    return matrix - np.diag(matrix.sum(axis=1))


STEP = -0.06 * derivative_matrix()


def slope(f, scale, ends=False):
    step = scale * STEP
    even_a, even_b, odd_a, odd_b = f[0] + f[4], f[1] + f[3], f[0] - f[4], f[1] - f[3]
    twice = f[2] + f[2]
    even_a, even_b = even_a - twice, even_b - twice
    out = [None] * 5
    for i in (0,) if ends else (0, 1):
        minus = float(step[i, 0] + step[i, 4]) * 0.5 * even_a + float(step[i, 1] + step[i, 3]) * 0.5 * even_b
        plus = float(step[i, 0] - step[i, 4]) * 0.5 * odd_a + float(step[i, 1] - step[i, 3]) * 0.5 * odd_b
        out[i], out[4 - i] = plus + minus, plus - minus
    if not ends:
        out[2] = float(step[2, 0]) * odd_a + float(step[2, 1]) * odd_b
    return out


def operate(src, dst, depth, scale=1.0, axis=None):
    for j in range(5):
        if axis == 1 and 0 < j < 4:
            continue
        line = [5 * j + i for i in range(5)]
        grad = slope([src[n] for n in line], scale, axis == 0)
        part = slope([src[25 + n] for n in line], scale, axis == 0)
        for i, n in enumerate(line):
            if grad[i] is not None:
                dst[25 + n] = depth(n) * grad[i]
                dst[n] = part[i]
    for i in range(5):
        if axis == 0 and 0 < i < 4:
            continue
        line = [5 * j + i for j in range(5)]
        grad = slope([src[n] for n in line], scale, axis == 1)
        part = slope([src[50 + n] for n in line], scale, axis == 1)
        for j, n in enumerate(line):
            if grad[j] is not None:
                dst[50 + n] = depth(n) * grad[j]
                dst[n] = dst[n] + part[j]


def weighted(values, weights):
    total = None
    for value, weight in zip(values, weights):
        value = value if weight == 1.0 else weight * value
        total = value if total is None else total + value
    return total


def lanes(x, by):
    return x if by % 128 == 0 else pltpu.roll(x, by % 128, 1)


def subs(x, by):
    return pltpu.roll(x, by % 8, 0)


class Grid:
    def __init__(self):
        self.lane = lax.broadcasted_iota(jnp.int32, (8, 128), 1)
        self.sub = lax.broadcasted_iota(jnp.int32, (8, 128), 0)
        self.col = self.lane % 32
        self.west = self.col < 16
        self.south = self.sub < 4

    def across(self, x, face):
        if face == 0:
            return lanes(x, 1)
        if face == 1:
            return lanes(x, -1)
        if face == 2:
            y = lanes(x, 32)
            return jnp.where(self.lane < 32, subs(y, 1), y)
        y = lanes(x, -32)
        return jnp.where(self.lane >= 96, subs(y, -1), y)


def spread_ints(ref, out):
    for j in range(8):
        out[:, j, :] = ref[:, 128 * j : 128 * j + 128]


def face_facts(near, owner, facts):
    me = lax.axis_index("curve")
    odd = me % 2
    chip = me + 1 - 2 * odd
    swap = me - 1 + 2 * odd
    for f in range(4):
        wall = near[f] < 0
        remote = (near[f] >= 0) & (owner[f] != me)
        peer = jnp.where(remote, owner[f], -1).astype(F32)
        peer = jnp.max(jnp.max(peer, axis=1, keepdims=True), axis=0, keepdims=True).astype(jnp.int32)
        peer = jnp.broadcast_to(peer, (8, 128))
        slot = jnp.where(peer == chip, 0, jnp.where(peer == swap, 1, 2))
        facts[f] = jnp.where(peer < 0, 3, slot)
        facts[4 + f] = jnp.where(wall, 1, jnp.where(remote, 2, 0))


def read_facts(facts):
    walls = [facts[4 + f] == 1 for f in range(4)]
    remotes = [facts[4 + f] == 2 for f in range(4)]
    return walls, remotes, [facts[f] for f in range(4)]


def flux(js, jn, jt, speed, depth, sign):
    lifted = LIFT * speed
    turn = LIFT * sign
    return lifted * js - turn * jn, lifted * jn - depth * (turn * js), lifted * jt


def side_edges(grid, get):
    blank = jnp.zeros((8, 128), F32)
    west, east = [blank] * 5, [blank] * 5
    for i in VALUES:
        a, by = divmod(i, 32)
        by = 2 * by if by < 16 else 2 * by - 31
        turned = lanes(get(i), by)
        west[a] = jnp.where(grid.col == by, turned, west[a])
        east[a] = jnp.where(grid.col == (31 + by) % 32, turned, east[a])
    return west, [lanes(x, -31) for x in east]


def row_edges(grid, ps):
    blank = jnp.zeros((8, 128), F32)
    south, north = [blank] * 5, [blank] * 5
    for group in range(IN_ALL // 8):
        a, g = divmod(group, 4)
        base = {13: 17, 14: 18, 15: 19, 16: 20, 17: 13, 18: 14}.get(group, group)
        here = grid.lane // 32 == g
        low = ps[pl.ds(64 * base, 8, stride=8), :]
        high = ps[pl.ds(64 * base + 7, 8, stride=8), :]
        south[a] = jnp.where(here, lanes(low, 32 * g), south[a])
        north[a] = jnp.where(here, lanes(high, 32 * g + 32), north[a])
    return south, north


def first_kernel(
    sea_in, dep_in, near_in, owner_in, cl_in, ex, eo, ps, u, tr1, tr2, nf, cc, facts, sea, dep, nb, ow, cl, near, owner, change, sems
):
    copies = [
        pltpu.make_async_copy(src, dst, sems.at[i])
        for i, (src, dst) in enumerate(((sea_in, sea), (dep_in, dep), (near_in, nb), (owner_in, ow), (cl_in, cl)))
    ]
    for copy in copies:
        copy.start()
    grid = Grid()
    lane, sub, col = grid.lane, grid.sub, grid.col
    for copy in copies[2:]:
        copy.wait()
    spread_ints(nb, near)
    spread_ints(ow, owner)
    face_facts(near, owner, facts)
    for copy in copies[:2]:
        copy.wait()
    walls, remotes, slots = read_facts(facts)
    inner = [~(walls[f] | remotes[f]) for f in range(4)]
    u[0] = sea[...].reshape(75, 8, 128)
    ps[8 * AT_DEPTH : 8 * AT_FLAG, :] = dep[...].reshape(25, 8, 128).reshape(200, 128)

    def put(p, value):
        ps[8 * p : 8 * p + 8, :] = value

    def get(p):
        return ps[8 * p : 8 * p + 8, :]

    def depth(n):
        return get(AT_DEPTH + n)

    for k in range(3):
        operate(u.at[k], u.at[k + 1], depth, RATIO[k])
    for v in range(3):
        for n in range(25):
            terms = [u[k, 25 * v + n] for k in range(4)]
            u[4, 25 * v + n] = weighted(terms, HALF)
            if n in PLACE:
                tr1[16 * v + PLACE[n]] = weighted(terms, HALF)
                tr2[16 * v + PLACE[n]] = weighted(terms, SECOND)
    operate(u.at[4], change, depth)
    for i in range(75):
        put(i, u[0, i] + change[i])
    for f in range(4):
        sign = -1.0 if f % 2 == 0 else 1.0
        normal, tangent = (1, 2) if f < 2 else (2, 1)
        echo = jnp.where(walls[f], -2.0, 0.0)
        for k in range(5):
            n, opposite = FACES[f][k], FACES[f ^ 1][k]
            a = [tr1[16 * v + PLACE[n]] for v in range(3)]
            b = [grid.across(tr1[16 * v + PLACE[opposite]], f) for v in range(3)]
            for v in range(3):
                nf[15 * f + 5 * v + k] = b[v]
            own = depth(n)
            other = jnp.where(inner[f], grid.across(depth(opposite), f), own)
            speed = jnp.sqrt(jnp.maximum(own, other))
            cc[5 * f + k] = speed
            js = jnp.where(inner[f], b[0] - a[0], 0.0)
            jn = jnp.where(inner[f], b[normal] - a[normal], echo * a[normal])
            jt = jnp.where(inner[f], b[tangent] - a[tangent], 0.0)
            out = flux(js, jn, jt, speed, own, sign)
            for v, part in ((0, out[0]), (normal, out[1]), (tangent, out[2])):
                put(25 * v + n, get(25 * v + n) + part)
    put(AT_FLAG, jnp.where(cl[...] == 0, 1.0, 0.0))
    for v in range(3):
        for k in range(5):
            i = 5 * v + k
            for src, x, y in ((tr1, AT_X, AT_Y), (tr2, AT_X2, AT_Y2)):
                at = [src[16 * v + PLACE[FACES[f][k]]] for f in range(4)]
                put(x + i, jnp.where(grid.west, at[0], at[1]))
                put(y + i, jnp.where(grid.south, at[2], at[3]))
    blank = jnp.zeros((8, 128), F32)
    corner = ((col == 0) | (col == 31)) & (((sub == 0) & (lane < 32)) | ((sub == 7) & (lane >= 96)))
    for which, at, low, high, mask in ((0, AT_Y, 2, 3, grid.south), (1, AT_X, 0, 1, grid.west)):
        total = blank
        for i in range(20):
            value = get(at + i) if i < 15 else jnp.where(mask, depth(FACES[low][i - 15]), depth(FACES[high][i - 15]))
            total = total + lanes(jnp.where(corner, value, 0.0), i)
        ex[5 + which] = total
        eo[5 + which] = total

    west, east = side_edges(grid, get)
    for slot, out in ((0, ex), (1, eo)):
        for a in range(5):
            out[a] = jnp.where(slots[0] == slot, west[a], east[a])
    turned = jnp.max(jnp.where((slots[2] < 2) | (slots[3] < 2), 1.0, 0.0)) > 0.5

    @pl.when(turned)
    def _():
        south, north = row_edges(grid, ps)
        for slot, out in ((0, ex), (1, eo)):
            for a in range(5):
                out[a] = jnp.where(slots[2] == slot, south[a], jnp.where(slots[3] == slot, north[a], out[a]))


def messages_kernel(ps, u, facts, es, cb, whole):
    grid = Grid()
    _, _, slots = read_facts(facts)
    south, north = row_edges(grid, ps)
    for a in range(5):
        es[a] = jnp.where(slots[2] == 2, south[a], north[a])
    for i in range(75):
        whole[i] = weighted([u[k, i] for k in range(4)], WHOLE)
    operate(whole, cb, lambda n: ps[8 * (AT_DEPTH + n) : 8 * (AT_DEPTH + n) + 8, :])
    for i in range(75):
        cb[i] = cb[i] + u[0, i]
    turned = jnp.max(jnp.where((slots[0] == 2) | (slots[1] == 2), 1.0, 0.0)) > 0.5

    @pl.when(turned)
    def _():
        west, east = side_edges(grid, lambda p: ps[8 * p : 8 * p + 8, :])
        for a in range(5):
            es[a] = jnp.where(slots[0] == 2, west[a], jnp.where(slots[1] == 2, east[a], es[a]))


def unpack_sides(grid, got, hx):
    for a in range(5):
        pair = (
            jnp.where(grid.lane % 2 == 0, got[0][a], lanes(got[1][a], 31)),
            jnp.where(grid.lane % 2 == 0, lanes(got[0][a], -1), lanes(got[1][a], 30)),
        )
        for i in VALUES:
            if i // 32 == a:
                hx[8 * i : 8 * i + 8, :] = lanes(pair[i % 32 // 16], -2 * (i % 16))


def touch(grid, axis, h, g, m, ps, masks, fast, before):
    first, last = 2 * axis, 2 * axis + 1
    normal, tangent = (2, 1) if axis else (1, 2)
    side, at = (grid.south, AT_Y) if axis else (grid.west, AT_X)
    sign = jnp.where(side, 1.0, -1.0)

    def get(p):
        return ps[8 * p : 8 * p + 8, :]

    def halo(p):
        return h[8 * p : 8 * p + 8, :]

    for i in range(75):
        g[0, i] = halo(i)
    for k in range(5):
        n, opposite = FACES[first][k], FACES[last][k]
        a = [halo(IN_FACE + 5 * v + k) for v in range(3)]
        b = [get(at + 5 * v + k) for v in range(3)]
        own = jnp.where(side, get(AT_DEPTH + n), get(AT_DEPTH + opposite))
        other = jnp.where(side, halo(AT_DEPTH + opposite), halo(AT_DEPTH + n))
        speed = jnp.sqrt(jnp.maximum(own, other))
        j = [b[v] - a[v] for v in range(3)]
        out = flux(j[0], j[normal], j[tangent], speed, other, sign)
        for v, part in ((0, out[0]), (normal, out[1]), (tangent, out[2])):
            g[0, 25 * v + opposite] = g[0, 25 * v + opposite] + jnp.where(side, part, 0.0)
            g[0, 25 * v + n] = g[0, 25 * v + n] + jnp.where(side, 0.0, part)
        out = flux(-j[0], -j[normal], -j[tangent], speed, own, -sign)
        for f in (first, last):
            node = FACES[f][k]
            fast[5 * f + k] = jnp.where(masks[f], speed, fast[5 * f + k])
            for v in range(3):
                before[15 * f + 5 * v + k] = jnp.where(masks[f], a[v], before[15 * f + 5 * v + k])
            for v, part in ((0, out[0]), (normal, out[1]), (tangent, out[2])):
                m[0, 25 * v + node] = m[0, 25 * v + node] + jnp.where(masks[f], part, 0.0)


def sides_kernel(rx, ro, facts, ps, nf, cc, hx, gx, m, before, fast):
    grid = Grid()
    _, remotes, slots = read_facts(facts)
    unpack_sides(grid, [[jnp.where(slots[f] == 0, rx[a], ro[a]) for a in range(5)] for f in (0, 1)], hx)
    for i in range(75):
        m[0, i] = ps[8 * i : 8 * i + 8, :]
    for i in range(60):
        before[i] = nf[i]
    for i in range(20):
        fast[i] = cc[i]
    touch(grid, 0, hx, gx, m, ps, [remotes[f] & (slots[f] != 2) for f in (0, 1)], fast, before)


def second_kernel(
    rx, ro, rs, ps, cb, tr1, tr2, facts, _hx, _gx, _m, _before, _fast, upd, se, so, hx, gx, m, before, fast, hy, gy, late, after
):
    grid = Grid()
    lane, sub = grid.lane, grid.sub
    walls, remotes, slots = read_facts(facts)

    def get(p):
        return ps[8 * p : 8 * p + 8, :]

    def depth(n):
        return get(AT_DEPTH + n)

    got = [
        [jnp.where(slots[f] == 0, rx[a], jnp.where(slots[f] == 1, ro[a], rs[a])) for a in range(5)] for f in range(4)
    ]
    turned = jnp.max(jnp.where((slots[0] == 2) | (slots[1] == 2), 1.0, 0.0)) > 0.5
    for group in range(IN_ALL // 8):
        a, q = divmod(group, 4)
        hy[pl.ds(64 * group, 8, stride=8), :] = lanes(got[2][a], -32 * q)
        hy[pl.ds(64 * group + 7, 8, stride=8), :] = lanes(got[3][a], 96 - 32 * q)

    def diagonal(f, h, which):
        slot = jnp.where(slots[f] == 2, slots[h], slots[f])
        return jnp.where(slot == 0, rs[5 + which], rs[7 + which])

    there = [[(slots[f] < 3) & (slots[h] < 3) for h in (2, 3)] for f in (0, 1)]
    low, high = sub == 0, sub == 7
    corners = []
    for which in (0, 1):
        corners.append(
            jnp.where(
                grid.south,
                subs(jnp.where(lane < 25, lanes(diagonal(0, 2, which), 1), lanes(diagonal(1, 2, which), 63)), 1),
                subs(
                    jnp.where(
                        (lane >= 96) & (lane < 120), lanes(diagonal(0, 3, which), 65), lanes(diagonal(1, 3, which), 127)
                    ),
                    -1,
                ),
            )
        )
    corner_w = (low & (lane == 0) & there[0][0]) | (high & (lane == 96) & there[0][1])
    corner_e = (low & (lane == 31) & there[1][0]) | (high & (lane == 127) & there[1][1])
    corner_s = low & (corner_w | corner_e)
    corner_n = high & (corner_w | corner_e)

    touch(grid, 1, hy, gy, m, ps, remotes, fast, before)

    @pl.when(turned)
    def _():
        unpack_sides(grid, got, hx)
        touch(grid, 0, hx, gx, m, ps, [remotes[f] & (slots[f] == 2) for f in (0, 1)], fast, before)

    for axis, h, g in ((1, hy, gy), (0, hx, gx)):
        first, last = 2 * axis, 2 * axis + 1
        normal, tangent = (2, 1) if axis else (1, 2)

        def halo(p, h=h):
            return h[8 * p : 8 * p + 8, :]

        def halo_depth(n, halo=halo):
            return halo(AT_DEPTH + n)

        first, last = 2 - first, 3 - first
        on_first, on_last = (corner_w, corner_e) if axis else (corner_s, corner_n)
        side = grid.west if axis else grid.south
        sign = jnp.where(side, -1.0, 1.0)
        for k in range(5):
            a = [halo(IN_SIDE + 5 * v + k) for v in range(3)]
            b = [lanes(corners[axis], -(5 * v + k)) for v in range(3)]
            own = jnp.where(side, halo_depth(FACES[first][k]), halo_depth(FACES[last][k]))
            speed = jnp.sqrt(jnp.maximum(own, lanes(corners[axis], -(15 + k))))
            j = [b[v] - a[v] for v in range(3)]
            out = flux(j[0], j[tangent], j[normal], speed, own, sign)
            for v, part in ((0, out[0]), (tangent, out[1]), (normal, out[2])):
                for f, mask in ((first, on_first), (last, on_last)):
                    at_node = 25 * v + FACES[f][k]
                    g[0, at_node] = g[0, at_node] + jnp.where(mask, part, 0.0)
        for k in range(3):
            operate(g.at[k], g.at[k + 1], halo_depth, RATIO[k], axis if k == 2 else None)
        side = grid.south if axis else grid.west
        halo_fine = halo(AT_FLAG) > 0.5
        for v in range(3):
            for k in range(5):
                n, opposite = FACES[2 * axis][k], FACES[2 * axis + 1][k]
                terms = [jnp.where(side, g[q, 25 * v + opposite], g[q, 25 * v + n]) for q in range(4)]
                after[15 * axis + 5 * v + k] = jnp.where(
                    halo_fine, weighted(terms, HALF), halo(IN_SECOND + 5 * v + k)
                )

    for k in range(3):
        operate(m.at[k], m.at[k + 1], depth, RATIO[k])
    for v in range(3):
        for n in range(25):
            value = weighted([m[k, 25 * v + n] for k in range(4)], HALF)
            m[4, 25 * v + n] = value
            if n in PLACE:
                late[16 * v + PLACE[n]] = value
    operate(m.at[4], m.at[1], depth)
    fine = get(AT_FLAG) > 0.5
    for i in range(75):
        upd[i] = jnp.where(fine, m[0, i] + m[1, i], cb[i])
    for f in range(4):
        sign = -1.0 if f % 2 == 0 else 1.0
        axis = f // 2
        normal, tangent = (2, 1) if axis else (1, 2)
        for k in range(5):
            n, opposite = FACES[f][k], FACES[f ^ 1][k]
            speed = fast[5 * f + k]
            j, a_list = [], []
            for v in range(3):
                at, across = 16 * v + PLACE[n], 16 * v + PLACE[opposite]
                a = jnp.where(fine, late[at], tr1[at] + tr2[at])
                sent = grid.across(jnp.where(fine, late[across], tr2[across]), f)
                sent = jnp.where(remotes[f], after[15 * axis + 5 * v + k], sent)
                b = jnp.where(fine, sent, before[15 * f + 5 * v + k] + sent)
                a_list.append(a)
                j.append(b - a)
            js = jnp.where(walls[f], 0.0, j[0])
            jn = jnp.where(walls[f], -2.0 * a_list[normal], j[normal])
            jt = jnp.where(walls[f], 0.0, j[tangent])
            out = flux(js, jn, jt, speed, depth(n), sign)
            for v, part in ((0, out[0]), (normal, out[1]), (tangent, out[2])):
                upd[25 * v + n] = upd[25 * v + n] + part
    even = (lane // 32) % 2 == 0
    for p in range(38):
        one = upd[2 * p]
        two = upd[min(2 * p + 1, 74)]
        se[p] = jnp.where(even, one, lanes(two, 32))
        so[p] = jnp.where(even, lanes(two, -32), one)


def settle_kernel(swap, re, upd, kept, take):
    grid = Grid()
    group = grid.lane // 32
    even = group % 2 == 0
    row = grid.sub * 4 + group
    moves = jnp.zeros((8, 128), jnp.int32)
    for b in range(32):
        moves = jnp.where(row == b, swap[b], moves)
    moves = moves > 0
    take[0] = jnp.where(moves & ~even, 1.0, 0.0)
    for i in range(75):
        e = lanes(re[i // 2], -32) if i % 2 else re[i // 2]
        kept[i] = jnp.where(moves & even, e, upd[i])


def third_kernel(ro, kept, take, out, buf, flat, sems):
    moves = take[0] > 0.5
    for v in range(3):
        for i in range(25 * v, 25 * v + 25):
            o = lanes(ro[i // 2], 32) if i % 2 else ro[i // 2]
            buf[i] = jnp.where(moves, o, kept[i])
        flat[v] = buf[25 * v : 25 * v + 25].reshape(25, 1024)
        pltpu.make_async_copy(flat.at[v], out.at[v], sems.at[v]).start()
    for v in range(3):
        pltpu.make_async_copy(flat.at[v], out.at[v], sems.at[v]).wait()


VM = pl.BlockSpec(memory_space=pltpu.VMEM)
ANY = pl.BlockSpec(memory_space=pltpu.HBM)
PARAMS = pltpu.CompilerParams(vmem_limit_bytes=40 * 1024 * 1024)


def in_hbm(x):
    return pltpu.with_memory_space_constraint(x, pltpu.HBM)


def planes(*counts):
    return [jax.ShapeDtypeStruct((c, 8, 128), F32) for c in counts]


def local(sea_state, water_depth, neighbours, neighbour_owner, clusters, block_swap):
    devices = lax.axis_size("curve")
    odd_swap = [(i, i + 1) for i in range(1, devices - 1, 2)] + [(i + 1, i) for i in range(1, devices - 1, 2)]
    chip_swap = [(i, i ^ 1) for i in range(devices)]
    far = devices // 2

    def passed(x, pairs):
        return lax.ppermute(x, "curve", pairs)

    ex, eo, ps, u, tr1, tr2, nf, cc, facts = pl.pallas_call(
        first_kernel,
        out_shape=planes(7, 7)
        + [jax.ShapeDtypeStruct((8 * PLANES, 128), F32), jax.ShapeDtypeStruct((5, 75, 8, 128), F32)]
        + planes(48, 48, 60, 20)
        + [jax.ShapeDtypeStruct((8, 8, 128), jnp.int32)],
        in_specs=[ANY] * 5,
        out_specs=[VM] * 9,
        scratch_shapes=[
            pltpu.VMEM((3, 25, 1024), F32),
            pltpu.VMEM((25, 1024), F32),
            pltpu.VMEM((4, 1024), jnp.int32),
            pltpu.VMEM((4, 1024), jnp.int32),
            pltpu.VMEM((8, 128), jnp.int32),
            pltpu.VMEM((4, 8, 128), jnp.int32),
            pltpu.VMEM((4, 8, 128), jnp.int32),
            pltpu.VMEM((75, 8, 128), F32),
            pltpu.SemaphoreType.DMA((5,)),
        ],
        compiler_params=PARAMS,
        name="predict",
    )(*(in_hbm(x) for x in (sea_state, water_depth, neighbours, neighbour_owner, clusters.reshape(8, 128))))
    es, cb = pl.pallas_call(
        messages_kernel,
        out_shape=planes(9, 75),
        in_specs=[VM] * 3,
        out_specs=[VM] * 2,
        scratch_shapes=[pltpu.VMEM((75, 8, 128), F32)],
        compiler_params=PARAMS,
        cost_estimate=pl.CostEstimate(flops=2_000_000, bytes_accessed=4_000_000, transcendentals=0),
        name="messages",
    )(ps, u, facts)
    ro = passed(eo, odd_swap)
    rx = passed(ex, chip_swap)
    es = lax.dynamic_update_slice(lax.dynamic_update_slice(es, ro[5:], (7, 0, 0)), rx[5:], (5, 0, 0))
    rs = passed(es, [(i, (i + far) % devices) for i in range(devices)])
    kept_on = [
        jax.ShapeDtypeStruct((8 * IN_ALL, 128), F32),
        jax.ShapeDtypeStruct((4, 75, 8, 128), F32),
        jax.ShapeDtypeStruct((5, 75, 8, 128), F32),
    ] + planes(60, 20)
    sides = pl.pallas_call(
        sides_kernel,
        out_shape=kept_on,
        in_specs=[VM] * 6,
        out_specs=[VM] * 5,
        compiler_params=PARAMS,
        cost_estimate=pl.CostEstimate(flops=2_000_000, bytes_accessed=4_000_000, transcendentals=0),
        name="sides",
    )(rx, ro, facts, ps, nf, cc)
    upd, se, so, *_ = pl.pallas_call(
        second_kernel,
        out_shape=planes(75, 38, 38) + kept_on,
        in_specs=[VM] * 13,
        out_specs=[VM] * 8,
        input_output_aliases={8 + i: 3 + i for i in range(5)},
        scratch_shapes=[
            pltpu.VMEM((8 * 160, 128), F32),
            pltpu.VMEM((4, 75, 8, 128), F32),
            pltpu.VMEM((48, 8, 128), F32),
            pltpu.VMEM((30, 8, 128), F32),
        ],
        compiler_params=PARAMS,
        name="correct",
    )(rx, ro, rs, ps, cb, tr1, tr2, facts, *sides)
    got_odd = passed(so, odd_swap)
    got_even = passed(se, chip_swap)
    kept, take = pl.pallas_call(
        settle_kernel,
        out_shape=planes(75, 1),
        in_specs=[pl.BlockSpec(memory_space=pltpu.SMEM)] + [VM] * 2,
        out_specs=[VM] * 2,
        compiler_params=PARAMS,
        cost_estimate=pl.CostEstimate(flops=2_000_000, bytes_accessed=4_000_000, transcendentals=0),
        name="settle",
    )(block_swap, got_even, upd)
    return pl.pallas_call(
        third_kernel,
        out_shape=jax.ShapeDtypeStruct((3, 25, 1024), F32),
        in_specs=[VM] * 3,
        out_specs=ANY,
        scratch_shapes=[
            pltpu.VMEM((75, 8, 128), F32),
            pltpu.VMEM((3, 25, 1024), F32),
            pltpu.SemaphoreType.DMA((3,)),
        ],
        compiler_params=PARAMS,
        name="migrate",
    )(got_odd, kept, take)


def solution(mesh):
    return jax.shard_map(
        local,
        mesh=mesh,
        in_specs=(
            P(None, None, "curve"),
            P(None, "curve"),
            P(None, "curve"),
            P(None, "curve"),
            P("curve"),
            P("curve"),
        ),
        out_specs=P(None, None, "curve"),
        check_vma=False,
    )
```
